256 devices in a mesh: pool: 32 (over x, z_hi, y), tp: 8 (over z_lo, core).
Axes of the slice: x: 4, y: 4, z: 8 (z_hi: 2, z_lo: 4; z = z_hi * 4 + z_lo), core: 2. Of those that a mesh axis runs over, the one named last changes fastest.
Arguments:
- queries: bfloat16 [16384, 4096], P('pool', 'tp'), may hold values from -400 to 400
- new_keys: bfloat16 [16384, 1024], P('pool', 'tp'), may hold values from -400 to 400
- new_values: bfloat16 [16384, 1024], P('pool', 'tp'), may hold values from -6 to 6
- kv_pool: bfloat16 [6144, 2, 64, 1024], P('pool', None, None, 'tp'), may hold values from -6 to 6
- out_weight: bfloat16 [4096, 4096], P('tp'), may hold values from -0.09375 to 0.09375
- prefix_len: int32 [32], P('pool'), may hold values from 1 to 8192
- new_count: int32 [32], P('pool'), may hold values from 1 to 512
- hit_holder: int32 [32, 128], P('pool'), may hold values from 0 to 31, as said below
- hit_block: int32 [32, 128], P('pool'), may hold values from 0 to 191
- decode_owner: int32 [32, 32], P('pool'), may hold values from 0 to 31, as said below
Outputs:
- projected: bfloat16 [16384, 4096], P(('pool', 'tp'))
- decode_pages: bfloat16 [32, 32, 1, 2, 16, 1024], P('pool', None, None, None, None, 'tp')
The draws below stay inside these ranges and needn't reach their ends.
Inputs may be any that keep to these rules, and one draw needn't show every extreme that they name: `hit_holder`: each request's 128 entries name every pool index exactly 4 times. `decode_owner`: each request's 32 entries name every pool index exactly 1 times.
All inputs are finite; a program needn't handle non-finite values.
Results may differ from the reference program's by a relative error of at most 0.017.
Values may be sent and summed in bfloat16 or wider, within the bound.
No kernel may reach another device: no remote copies, remote signals or barrier semaphores. Data moves between devices by JAX's collectives and lax.ppermute only.
A program may use at most 128 MiB of HBM per device.

```python
import jax
import jax.numpy as jnp
from jax import lax

HD = 128
QH = 32
KVH = 8
D_OUT = 4096
NEW = 512
BLK = 64
PB = 128
POOL_BLK = 192
PG = 16
REQUESTS = 32
TOKENS = 16384
CAP = 4
PAGES = 32
PCAP = 1
POOL_ALL = 6144
N_POOL = 32
N_TP = 8


def common_rows(key):
    keys = jax.random.split(key, 2)
    base_q = jnp.clip(jax.random.normal(keys[0], (TOKENS, QH * HD), jnp.float32), -5.0, 5.0)
    base_k = jnp.clip(jax.random.normal(keys[1], (TOKENS, KVH * HD), jnp.float32), -5.0, 5.0)
    return (base_q, base_k)


def draw_queries(key, part):
    base_q, base_k = common_rows(key)
    return base_q.astype(jnp.bfloat16)


def draw_new_keys(key, part):
    base_q, base_k = common_rows(key)
    return base_k.astype(jnp.bfloat16)


def spread_rows(key, rows, length, repeat):
    row_keys = jax.random.split(key, rows)
    base = jnp.tile(jnp.arange(length // repeat, dtype=jnp.int32), repeat)
    return jax.vmap(lambda single: jax.random.permutation(single, base))(row_keys).astype(jnp.int32)


def draw_hit_holder(key, part):
    key = jax.random.fold_in(key, 3)
    return spread_rows(key, REQUESTS, PB, CAP)


def draw_decode_owner(key, part):
    key = jax.random.fold_in(key, 5)
    return spread_rows(key, REQUESTS, PAGES, PCAP)


def set_ends(values, key, low, top_value):
    longest = values.shape.index(max(values.shape))
    spots = []
    for shift in (0, 1):
        where = [jax.random.randint(jax.random.fold_in(key, axis), (), 0, length) for axis, length in enumerate(values.shape)]
        where[longest] = (where[longest] + shift) % values.shape[longest]
        spots.append(tuple(where))
    return values.at[spots[0]].set(low).at[spots[1]].set(top_value)


def levels(rng, extent, cuts, smallest, largest):
    level = 1.0
    for dim, parts in cuts:
        steps = jax.random.uniform(jax.random.fold_in(jax.random.fold_in(rng, 6), dim), (parts,), jnp.float32, smallest / len(cuts), largest / len(cuts))
        level = level * jnp.repeat(jnp.exp(steps), extent[dim] // parts).reshape((-1,) + (1,) * (len(extent) - 1 - dim))
    return level


def gaussian(own_key, shape, scale, reach, shards=(), kind=jnp.bfloat16):
    values = jax.random.normal(own_key, shape, jnp.float32) * scale
    if len(shards) > 0:
        values = levels(own_key, shape, shards, -0.22, 0.18) * values
    return jnp.clip(values, min=-reach, max=reach).astype(kind)


def setup_inputs(seed: int = 0) -> dict:
    seeds = jax.random.split(jax.random.key(seed), 11)
    return {
        "queries": draw_queries(jax.random.fold_in(seeds[10], 71), 0),
        "new_keys": draw_new_keys(jax.random.fold_in(seeds[10], 71), 0),
        "new_values": gaussian(seeds[2], (TOKENS, KVH * HD), 1.0, 6.0, ((0, 32), (1, 8))),
        "kv_pool": gaussian(seeds[3], (POOL_ALL, 2, BLK, KVH * HD), 1.0, 6.0, ((0, 32), (3, 8))),
        "out_weight": gaussian(seeds[4], (QH * HD, D_OUT), (QH * HD) ** -0.5, 0.09375, ((0, 8),)),
        "prefix_len": set_ends(jax.random.randint(seeds[5], (REQUESTS,), 1, PB * BLK + 1), jax.random.fold_in(seeds[5], 1), 1, PB * BLK).astype(jnp.int32),
        "new_count": set_ends(jax.random.randint(seeds[6], (REQUESTS,), 1, NEW + 1), jax.random.fold_in(seeds[6], 1), 1, NEW).astype(jnp.int32),
        "hit_holder": draw_hit_holder(jax.random.fold_in(seeds[10], 71), 0),
        "hit_block": set_ends(jax.random.randint(seeds[8], (REQUESTS, PB), 0, POOL_BLK), jax.random.fold_in(seeds[8], 1), 0, POOL_BLK - 1).astype(jnp.int32),
        "decode_owner": draw_decode_owner(jax.random.fold_in(seeds[10], 71), 0),
    }


def reference(queries, new_keys, new_values, kv_pool, out_weight, prefix_len, new_count, hit_holder, hit_block, decode_owner):
    group = QH // KVH
    scale = HD ** -0.5
    slot = (hit_holder * POOL_BLK + hit_block).astype(jnp.int32)
    token = jnp.arange(NEW, dtype=jnp.int32)
    causal = token[None, :] <= token[:, None]

    def one_request(r):
        start = (r * NEW).astype(jnp.int32)
        query_rows = lax.dynamic_slice_in_dim(queries, start, NEW, 0).reshape(NEW, KVH, group, HD)
        key_rows = lax.dynamic_slice_in_dim(new_keys, start, NEW, 0).reshape(NEW, KVH, HD)
        value_rows = lax.dynamic_slice_in_dim(new_values, start, NEW, 0).reshape(NEW, KVH, HD)
        blocks = kv_pool[slot[r]]
        prefix_keys = blocks[:, 0].reshape(PB * BLK, KVH, HD)
        prefix_values = blocks[:, 1].reshape(PB * BLK, KVH, HD)
        keys = jnp.concatenate([prefix_keys, key_rows], axis=0)
        values = jnp.concatenate([prefix_values, value_rows], axis=0)
        prefix_ok = jnp.arange(PB * BLK, dtype=jnp.int32) < prefix_len[r]
        allowed = jnp.concatenate([jnp.broadcast_to(prefix_ok[None, :], (NEW, PB * BLK)), causal], axis=1)

        def one_head(g):
            query_head = query_rows[:, g].astype(jnp.float32)
            key_head = keys[:, g].astype(jnp.float32)
            value_head = values[:, g].astype(jnp.float32)
            scores = jnp.einsum("tjd,kd->tjk", query_head, key_head) * scale
            scores = jnp.where(allowed[:, None, :], scores, -jnp.inf)
            peak = jnp.max(scores, axis=2, keepdims=True)
            weights = jnp.exp(scores - peak)
            total = jnp.sum(weights, axis=2, keepdims=True)
            rounded = lax.optimization_barrier(weights.astype(jnp.bfloat16))
            mixed = jnp.einsum("tjk,kd->tjd", rounded.astype(jnp.float32), value_head) / total
            return mixed.astype(jnp.bfloat16)

        heads = lax.map(one_head, jnp.arange(KVH, dtype=jnp.int32))
        attention = jnp.transpose(heads, (1, 0, 2, 3)).reshape(NEW, QH * HD)
        keep = token < new_count[r]
        return jnp.where(keep[:, None], attention, jnp.zeros_like(attention))

    attention = lax.map(one_request, jnp.arange(REQUESTS, dtype=jnp.int32)).reshape(TOKENS, QH * HD)
    width = QH * HD // N_TP
    summed = jnp.zeros((TOKENS, D_OUT), jnp.float32)
    for part_index in range(N_TP):
        partial_value = jnp.dot(attention[:, part_index * width:(part_index + 1) * width], out_weight[part_index * width:(part_index + 1) * width], preferred_element_type=jnp.float32).astype(jnp.bfloat16)
        summed = summed + partial_value.astype(jnp.float32)
    projected = summed.astype(jnp.bfloat16)

    live_rows = token[None, :] < new_count[:, None]
    both = jnp.stack([new_keys.reshape(REQUESTS, NEW, KVH * HD), new_values.reshape(REQUESTS, NEW, KVH * HD)], axis=1)
    both = jnp.where(live_rows[:, None, :, None], both, jnp.zeros_like(both))
    pages = jnp.transpose(both.reshape(REQUESTS, 2, PAGES, PG, KVH * HD), (0, 2, 1, 3, 4))
    order = jnp.argsort(decode_owner, axis=1, stable=True).astype(jnp.int32)
    ordered = jax.vmap(lambda items, picks: items[picks])(pages, order)
    decode_pages = jnp.transpose(ordered.reshape(REQUESTS, N_POOL, PCAP, 2, PG, KVH * HD), (1, 0, 2, 3, 4, 5))
    return projected, decode_pages
```

```python
import functools
import jax
import jax.numpy as jnp
from jax import lax
from jax.experimental import pallas as pl
from jax.experimental.pallas import tpu as pltpu

HD = 128
NEG = -1e30
VMEM_LIMIT = 50 * 1024 * 1024
LOG2E = 1.4426950408889634


def tile_lanes(x, times):
    return x if times == 1 else jnp.concatenate([x] * times, axis=1)


def softmax_step(q, k, v, ok, m_prev, l_prev, acc_prev):
    c = HD ** (-0.5) * LOG2E
    width = k.shape[0] // HD
    s = lax.dot_general(q, k, (((1,), (1,)), ((), ())), preferred_element_type=jnp.float32)
    if ok is not None:
        s = jnp.where(ok, s, NEG)
    m_next = jnp.maximum(m_prev, jnp.max(s, axis=1, keepdims=True))
    p = jnp.exp2((s - tile_lanes(m_next, width)) * c)
    if ok is not None:
        p = jnp.where(ok, p, 0.0)
    alpha = jnp.exp2((m_prev - m_next) * c)
    part = p[:, :HD]
    for i in range(1, width):
        part = part + p[:, i * HD : (i + 1) * HD]
    mixed = jnp.dot(p.astype(jnp.bfloat16), v, preferred_element_type=jnp.float32)
    return m_next, alpha * l_prev + part, alpha * acc_prev + mixed


def prefix_pass(tab, q_ref, kv_hbm, kbuf, vbuf, acc, m_s, l_s, order, sems, ck, tb):
    holders, _, _, bl, _ = kv_hbm.shape
    n = order.shape[0]
    each = n // holders
    heads, tokens, _ = acc.shape
    per = ck // bl
    length, count = tab[n], tab[n + 1]

    def classify(i, carry):
        full, partial = carry
        left = length - tab[i] * bl

        @pl.when(left >= bl)
        def _():
            order[full] = i

        return (
            full + (left >= bl).astype(jnp.int32),
            jnp.where((left > 0) & (left < bl), i, partial),
        )

    full, partial = lax.fori_loop(0, n, classify, (jnp.int32(0), jnp.int32(-1)))
    has = (partial >= 0).astype(jnp.int32)

    @pl.when(partial >= 0)
    def _():
        order[full] = partial

    blocks = full + has
    rest = jnp.where(has > 0, length - tab[jnp.maximum(partial, 0)] * bl, 0)
    keys = full * bl + rest
    chunks = (blocks + per - 1) // per

    def load(i, carry):
        src = jnp.where(i < blocks, order[jnp.minimum(i, blocks - 1)], 0)
        at = pl.ds(pl.multiple_of(i * bl, bl), bl)
        pltpu.make_async_copy(kv_hbm.at[src // each, src % each, 0], kbuf.at[at], sems.at[0, i // per]).start()
        pltpu.make_async_copy(kv_hbm.at[src // each, src % each, 1], vbuf.at[at], sems.at[1, i // per]).start()
        return carry

    lax.fori_loop(0, chunks * per, load, 0)
    live_blocks = (count + tb - 1) // tb

    def one_chunk(ci, carry):
        at = pl.ds(pl.multiple_of(ci * ck, ck), ck)
        pltpu.make_async_copy(kbuf.at[at], kbuf.at[at], sems.at[0, ci]).wait()
        pltpu.make_async_copy(vbuf.at[at], vbuf.at[at], sems.at[1, ci]).wait()

        def rows(t, masked):
            k, v = kbuf[at], vbuf[at]
            ok = None
            if masked:
                ok = lax.broadcasted_iota(jnp.int32, (tb, ck), 1) < keys - ci * ck
            tok = pl.ds(pl.multiple_of(t * tb, tb), tb)
            for g in range(heads):
                m, l, a = softmax_step(
                    q_ref[tok, g * HD : (g + 1) * HD], k, v, ok,
                    m_s[g, tok], l_s[g, tok], acc[g, tok],
                )
                m_s[g, tok], l_s[g, tok], acc[g, tok] = m, l, a

        whole = keys >= (ci + 1) * ck

        @pl.when(whole)
        def _():
            lax.fori_loop(0, live_blocks, lambda t, x: (rows(t, False), x)[1], 0)

        @pl.when(jnp.logical_not(whole))
        def _():
            lax.fori_loop(0, live_blocks, lambda t, x: (rows(t, True), x)[1], 0)

        return carry

    lax.fori_loop(0, chunks, one_chunk, 0)


def reset(acc, m_s, l_s):
    acc[...] = jnp.zeros_like(acc)
    l_s[...] = jnp.zeros_like(l_s)
    m_s[...] = jnp.full_like(m_s, NEG)


def partner_kernel(tab, q_ref, kv_hbm, o_ref, st_ref, kbuf, vbuf, acc, m_s, l_s, order, sems, *, ck, tb):
    reset(acc, m_s, l_s)
    prefix_pass(tab, q_ref, kv_hbm, kbuf, vbuf, acc, m_s, l_s, order, sems, ck, tb)
    heads = acc.shape[0]
    lane = lax.broadcasted_iota(jnp.int32, m_s.shape[1:], 1)
    st = jnp.zeros(m_s.shape[1:], jnp.float32)
    for g in range(heads):
        total = jnp.sum(l_s[g], axis=1, keepdims=True)
        safe = jnp.where(total > 0, total, 1.0)
        o_ref[:, g * HD : (g + 1) * HD] = (acc[g] / safe).astype(o_ref.dtype)
        st = jnp.where(lane == g, m_s[g], st)
        st = jnp.where(lane == heads + g, total, st)
    st_ref[...] = st.T[: 2 * heads]


def scratch(n, heads, tokens, bl, ck):
    keys = n * bl
    return [
        pltpu.VMEM((keys, HD), jnp.bfloat16),
        pltpu.VMEM((keys, HD), jnp.bfloat16),
        pltpu.VMEM((heads, tokens, HD), jnp.float32),
        pltpu.VMEM((heads, tokens, HD), jnp.float32),
        pltpu.VMEM((heads, tokens, HD), jnp.float32),
        pltpu.SMEM((n,), jnp.int32),
        pltpu.SemaphoreType.DMA((2, keys // ck)),
    ]


VM = pl.BlockSpec(memory_space=pltpu.VMEM)
SM = pl.BlockSpec(memory_space=pltpu.SMEM)
ANY = pl.BlockSpec(memory_space=pl.ANY)


def partner_attention(tab, q, kv, ck=512, tb=256):
    n, bl = tab.shape[0] - 2, kv.shape[3]
    tokens, width = q.shape
    heads = width // HD
    return pl.pallas_call(
        functools.partial(partner_kernel, ck=ck, tb=tb),
        out_shape=[
            jax.ShapeDtypeStruct((tokens, width), jnp.bfloat16),
            jax.ShapeDtypeStruct((2 * heads, tokens), jnp.float32),
        ],
        in_specs=[SM, VM, ANY],
        out_specs=[VM, VM],
        scratch_shapes=scratch(n, heads, tokens, bl, ck),
        compiler_params=pltpu.CompilerParams(vmem_limit_bytes=VMEM_LIMIT),
        cost_estimate=pl.CostEstimate(
            flops=4 * tokens * width * n * bl, bytes_accessed=kv.size * 2, transcendentals=tokens * heads * n * bl
        ),
    )(tab, q, kv)


def causal_kernel(q_ref, k_ref, v_ref, o_ref, st_ref):
    tokens, width = q_ref.shape
    heads = width // HD
    c = HD ** (-0.5) * LOG2E
    ok = lax.broadcasted_iota(jnp.int32, (tokens, tokens), 1) <= lax.broadcasted_iota(
        jnp.int32, (tokens, tokens), 0
    )
    lane = lax.broadcasted_iota(jnp.int32, (tokens, HD), 1)
    st = jnp.zeros((tokens, HD), jnp.float32)
    for g in range(heads):
        s = lax.dot_general(
            q_ref[:, g * HD : (g + 1) * HD], k_ref[...], (((1,), (1,)), ((), ())),
            preferred_element_type=jnp.float32,
        )
        s = jnp.where(ok, s, NEG)
        m = jnp.max(s, axis=1, keepdims=True)
        p = jnp.where(ok, jnp.exp2((s - m) * c), 0.0)
        total = jnp.sum(p, axis=1, keepdims=True)
        mixed = jnp.dot(p.astype(jnp.bfloat16), v_ref[...], preferred_element_type=jnp.float32)
        o_ref[:, g * HD : (g + 1) * HD] = mixed / total
        st = jnp.where(lane == g, m, st)
        st = jnp.where(lane == heads + g, total, st)
    st_ref[...] = st.T[: 2 * heads]


def causal_attention(q, k, v):
    tokens, width = q.shape
    heads = width // HD
    return pl.pallas_call(
        causal_kernel,
        out_shape=[
            jax.ShapeDtypeStruct((tokens, width), jnp.float32),
            jax.ShapeDtypeStruct((2 * heads, tokens), jnp.float32),
        ],
        in_specs=[VM] * 3,
        out_specs=[VM] * 2,
        compiler_params=pltpu.CompilerParams(vmem_limit_bytes=VMEM_LIMIT),
        cost_estimate=pl.CostEstimate(
            flops=4 * tokens * width * tokens, bytes_accessed=tokens * width * 8, transcendentals=tokens * heads * tokens
        ),
    )(q, k, v)


def own_kernel(
    tab, q_ref, kv_hbm, op_ref, stp_ref, oc_ref, stc_ref, o_ref,
    kbuf, vbuf, acc, m_s, l_s, order, sems, *, ck, tb,
):
    reset(acc, m_s, l_s)
    prefix_pass(tab, q_ref, kv_hbm, kbuf, vbuf, acc, m_s, l_s, order, sems, ck, tb)
    heads, tokens, _ = acc.shape
    n = order.shape[0]
    c = HD ** (-0.5) * LOG2E
    fill = jnp.zeros((HD - 2 * heads, tokens), jnp.float32)
    stp = jnp.concatenate([stp_ref[...], fill], axis=0).T
    stc = jnp.concatenate([stc_ref[...], fill], axis=0).T
    alive = lax.broadcasted_iota(jnp.int32, (tokens, HD), 0) < tab[n + 1]
    for g in range(heads):
        cols = slice(g * HD, (g + 1) * HD)
        m_p, l_p = stp[:, g : g + 1], stp[:, heads + g : heads + g + 1]
        m_c, l_c = stc[:, g : g + 1], stc[:, heads + g : heads + g + 1]
        m_o = m_s[g][:, :1]
        l_o = jnp.sum(l_s[g], axis=1, keepdims=True)
        m = jnp.maximum(jnp.maximum(m_o, m_p), m_c)
        w_o = jnp.exp2((m_o - m) * c)
        w_p = l_p * jnp.exp2((m_p - m) * c)
        w_c = l_c * jnp.exp2((m_c - m) * c)
        inv = 1.0 / (l_o * w_o + w_p + w_c)
        mixed = (
            acc[g] * (w_o * inv)
            + op_ref[:, cols].astype(jnp.float32) * (w_p * inv)
            + oc_ref[:, cols] * (w_c * inv)
        )
        o_ref[:, cols] = jnp.where(alive, mixed, 0.0).astype(o_ref.dtype)


def own_attention(tab, q, kv, op, stp, oc, stc, ck=1024, tb=256):
    n, bl = tab.shape[0] - 2, kv.shape[3]
    tokens, width = q.shape
    heads = width // HD
    return pl.pallas_call(
        functools.partial(own_kernel, ck=ck, tb=tb),
        out_shape=jax.ShapeDtypeStruct((tokens, width), jnp.bfloat16),
        in_specs=[SM, VM, ANY, VM, VM, VM, VM],
        out_specs=VM,
        scratch_shapes=scratch(n, heads, tokens, bl, ck),
        compiler_params=pltpu.CompilerParams(vmem_limit_bytes=VMEM_LIMIT),
        cost_estimate=pl.CostEstimate(
            flops=4 * tokens * width * n * bl, bytes_accessed=kv.size * 2, transcendentals=tokens * heads * n * bl
        ),
    )(tab, q, kv, op, stp, oc, stc)


def gather_kernel(dest, ids, pool_ref, out_ref, sem):
    n, per = out_ref.shape[0], ids.shape[1]

    def one(i, carry):
        for k in range(per):
            pltpu.make_async_copy(pool_ref.at[ids[dest[i], k]], out_ref.at[i, k], sem).start()
        return carry

    lax.fori_loop(0, n, one, 0)
    pltpu.make_async_copy(out_ref, out_ref, sem).wait()


def gather_paged_kernel(dest, ids, pool_ref, near_ref, away_ref, out_ref, sems):
    n, per = out_ref.shape[0], ids.shape[1]
    half = near_ref.shape[1]

    def one(i, carry):
        for k in range(per):
            pltpu.make_async_copy(pool_ref.at[ids[dest[i], k]], out_ref.at[i, k], sems.at[0]).start()
        return carry

    lax.fori_loop(0, n, one, 0)
    for i in range(n):
        out_ref[i, per, 0, :half] = near_ref[i]
        out_ref[i, per, 0, half:] = away_ref[i]
        out_ref[i, per, 1] = jnp.zeros_like(out_ref[i, per, 1])
    filled = out_ref.at[:, pl.ds(0, per)]
    pltpu.make_async_copy(filled, filled, sems.at[0]).wait()


def gather_blocks(dest, ids, pool, pages=()):
    n, per = dest.shape[0], ids.shape[1]
    _, two, bl, _ = pool.shape
    return pl.pallas_call(
        gather_paged_kernel if pages else gather_kernel,
        out_shape=jax.ShapeDtypeStruct((n, per + (1 if pages else 0), two, bl, HD), pool.dtype),
        in_specs=[SM, SM, ANY] + [VM] * len(pages),
        out_specs=VM,
        scratch_shapes=[pltpu.SemaphoreType.DMA((1,)) if pages else pltpu.SemaphoreType.DMA],
        compiler_params=pltpu.CompilerParams(vmem_limit_bytes=VMEM_LIMIT),
        cost_estimate=pl.CostEstimate(flops=0, bytes_accessed=4 * n * per * two * bl * HD, transcendentals=0),
    )(dest, ids, pool, *pages)


NX, NZ, NY = 4, 2, 4
NL = 4
PG = 16


def by_rank(holders, per):
    slots = holders.shape[0]
    i = jnp.arange(slots, dtype=jnp.int32)
    same = (holders[:, None] == holders[None, :]) & (i[None, :] < i[:, None])
    place = holders * per + jnp.sum(same.astype(jnp.int32), axis=1)
    return place[None, :] == i[:, None]


def pick(hot, values):
    return jnp.sum(jnp.where(hot, values[None, :], 0), axis=1)


def local(
    queries,
    new_keys,
    new_values,
    kv_pool,
    out_weight,
    prefix_len,
    new_count,
    hit_holder,
    hit_block,
    decode_owner,
):
    slots = hit_holder.shape[1]
    n_pool = lax.axis_size("pool")
    per = slots // n_pool
    tokens, width = queries.shape
    plane_n = NX * NY
    me = lax.axis_index("pool")
    t_me = lax.axis_index("tp")
    zh = (me // NY) % NZ
    flip = [(p, p ^ NY) for p in range(n_pool)]
    planes = [[x * NZ * NY + z * NY + y for x in range(NX) for y in range(NY)] for z in range(NZ)]

    def a2a(x, groups=None):
        return lax.all_to_all(x, "pool", 0, 0, axis_index_groups=groups, tiled=True)

    hot = by_rank(hit_holder[0], per)
    slot_of = pick(hot, jnp.arange(slots, dtype=jnp.int32))
    ids = pick(hot, hit_block[0]).reshape(n_pool, per)
    ids_in = a2a(ids)
    lens = jnp.concatenate([prefix_len, new_count])
    meta = jnp.concatenate([slot_of, lens])
    q_far = lax.ppermute(queries, "pool", flip)
    meta_far = lax.ppermute(meta, "pool", flip)

    def table(info):
        grid = info[:slots].reshape(NX, NZ, NY * per)
        pos = lax.dynamic_index_in_dim(grid, zh, 1, keepdims=False).reshape(-1)
        return jnp.concatenate([pos, info[slots:]])

    keep = (jnp.arange(tokens, dtype=jnp.int32) < new_count[0])[:, None]
    both = jnp.stack([jnp.where(keep, new_keys, 0), jnp.where(keep, new_values, 0)])
    pages = decode_owner.shape[1]
    both = both.reshape(2, pages, PG, HD)
    page_of = pick(by_rank(decode_owner[0], 1), jnp.arange(pages, dtype=jnp.int32))
    ordered = jnp.transpose(both[:, page_of], (1, 0, 2, 3)).reshape(NX, NZ, NY, 2 * PG, HD)
    near = lax.dynamic_index_in_dim(ordered, zh, 1, keepdims=False).reshape(plane_n, 2 * PG, HD)
    away = lax.dynamic_index_in_dim(ordered, 1 - zh, 1, keepdims=False).reshape(plane_n, 2 * PG, HD)
    away = lax.ppermute(away, "pool", flip)

    xs, ys = jnp.arange(plane_n, dtype=jnp.int32) // NY, jnp.arange(plane_n, dtype=jnp.int32) % NY
    base = xs * (NZ * NY) + ys
    send_far = gather_blocks(base + (1 - zh) * NY, ids_in, kv_pool)
    send_own = gather_blocks(base + zh * NY, ids_in, kv_pool, (near, away))
    send_own, q_far = lax.optimization_barrier((send_own, q_far))
    got_far = a2a(send_far, planes)
    got_own = a2a(send_own, planes)

    o_c, st_c = causal_attention(queries, new_keys, new_values)
    w_other = lax.ppermute(out_weight, "tp", [(t, t ^ 1) for t in range(2 * NL)])

    tab_far = table(meta_far)
    o_far, st_far = partner_attention(tab_far, q_far, got_far, ck=1024)
    o_p = lax.ppermute(o_far, "pool", flip)
    st_p = lax.ppermute(st_far, "pool", flip)

    att = own_attention(table(meta), queries, got_own, o_p, st_p, o_c, st_c)

    core, j = t_me % 2, t_me // 2
    rows = att.reshape(NL, 2, tokens // (2 * NL), width)
    x_me = lax.dynamic_index_in_dim(rows, core, 1, keepdims=False)
    x_give = lax.dynamic_index_in_dim(rows, 1 - core, 1, keepdims=False)
    x_got = lax.ppermute(x_give, "tp", [(t, t ^ 1) for t in range(2 * NL)])
    d_out = out_weight.shape[1]
    chunk = tokens // (2 * NL)
    part = jnp.dot(x_me.reshape(-1, width), out_weight, preferred_element_type=jnp.float32)
    part = part + jnp.dot(x_got.reshape(-1, width), w_other, preferred_element_type=jnp.float32)
    part = part.astype(jnp.bfloat16).reshape(NL, chunk, d_out)

    def own_part(d):
        d = jnp.clip(d, 0, NL - 1)
        return lax.dynamic_index_in_dim(part, d, 0, keepdims=False).astype(jnp.float32)

    right = left = None
    for s in range(1, NL):
        give_r, give_l = own_part(NL - s + j), own_part(s + j - NL)
        if right is not None:
            give_r, give_l = give_r + right.astype(jnp.float32), give_l + left.astype(jnp.float32)
        hops = [(jj, jj + 1) for jj in range(s)]
        to_r = [(2 * a + k, 2 * b + k) for a, b in hops for k in range(2)]
        to_l = [(2 * (NL - 1 - a) + k, 2 * (NL - 1 - b) + k) for a, b in hops for k in range(2)]
        right = lax.ppermute(give_r.astype(jnp.bfloat16), "tp", to_r)
        left = lax.ppermute(give_l.astype(jnp.bfloat16), "tp", to_l)
    summed = own_part(j) + right.astype(jnp.float32) + left.astype(jnp.float32)

    arrived = got_own[:, per, 0].reshape(NX, NY, 2, 2 * PG, HD)
    near_in, far_in = arrived[:, :, 0], arrived[:, :, 1]
    by_z = jnp.where(zh == 0, jnp.stack([near_in, far_in], 1), jnp.stack([far_in, near_in], 1))
    decode = by_z.reshape(n_pool, 1, 2, PG, HD)[None]
    return (summed.astype(jnp.bfloat16), decode)


def solution(mesh):
    from jax.sharding import PartitionSpec as P

    in_specs = (
        P("pool", "tp"),
        P("pool", "tp"),
        P("pool", "tp"),
        P("pool", None, None, "tp"),
        P("tp", None),
        P("pool"),
        P("pool"),
        P("pool", None),
        P("pool", None),
        P("pool", None),
    )
    out_specs = (P(("pool", "tp"), None), P("pool", None, None, None, None, "tp"))
    return jax.shard_map(local, mesh=mesh, in_specs=in_specs, out_specs=out_specs, check_vma=False)
```

```python
import functools

import jax
import jax.numpy as jnp
from jax import lax
from jax.experimental import pallas as pl
from jax.experimental.pallas import tpu as pltpu
from jax.sharding import PartitionSpec as P

HD = 128
PG = 16
NX, NZ, NY = 4, 2, 4
NL = 4
SENDS = ((0, 2, 3, 1), (1, 0, 2, 3), (2, 3, 1, 0), (3, 1, 0, 2))
CK = 1024
NEG = -1e30
VMEM_LIMIT = 50 * 1024 * 1024
RATE = HD ** (-0.5) * 1.4426950408889634

VM = pl.BlockSpec(memory_space=pltpu.VMEM)
SM = pl.BlockSpec(memory_space=pltpu.SMEM)
ANY = pl.BlockSpec(memory_space=pl.ANY)
PARAMS = pltpu.CompilerParams(vmem_limit_bytes=VMEM_LIMIT)


def plan_kernel(holder, block, prefix_len, new_count, out):
    n = out.shape[0]
    slots = holder.shape[1]
    per = slots // n
    hit = lax.broadcasted_iota(jnp.int32, (n, slots), 0) == holder[...]
    lane = lax.broadcasted_iota(jnp.int32, (slots, slots), 1)
    earlier = (lax.broadcasted_iota(jnp.int32, (slots, slots), 0) < lane).astype(jnp.float32)
    rank = jnp.dot(hit.astype(jnp.float32), earlier, preferred_element_type=jnp.float32)
    at = lax.broadcasted_iota(jnp.int32, (n, out.shape[1]), 1)
    spot = lax.broadcasted_iota(jnp.int32, (n, slots), 1)
    ids = jnp.broadcast_to(block[...], (n, slots))
    row = jnp.where(at == 2 * per, prefix_len[0], 0) + jnp.where(at == 2 * per + 1, new_count[0], 0)
    for k in range(per):
        one = hit & (rank == k)
        row = jnp.where(at == k, jnp.sum(jnp.where(one, ids, 0), axis=1, keepdims=True), row)
        row = jnp.where(at == per + k, jnp.sum(jnp.where(one, spot, 0), axis=1, keepdims=True), row)
    out[...] = row


def plan(hit_holder, hit_block, prefix_len, new_count, n_pool):
    return pl.pallas_call(
        plan_kernel,
        out_shape=jax.ShapeDtypeStruct((n_pool, HD), jnp.int32),
        in_specs=[VM, VM, SM, SM],
        out_specs=VM,
        cost_estimate=pl.CostEstimate(flops=2 * n_pool * HD * HD, bytes_accessed=n_pool * HD * 4, transcendentals=0),
    )(hit_holder, hit_block, prefix_len, new_count)


def block_table(info, zh, per, ranks, bl):
    grid = info[:, per : 2 * per].reshape(NX, NZ, NY, per)
    pos = lax.dynamic_index_in_dim(grid, zh, 1, keepdims=False).reshape(NX * NY, per)
    pos = pos[:, ranks[0] : ranks[1]].reshape(-1)
    n = pos.shape[0]
    i = jnp.arange(n, dtype=jnp.int32)
    code = (i // (ranks[1] - ranks[0])) * 16 + i % (ranks[1] - ranks[0])
    live = jnp.clip(info[0, 2 * per] - pos * bl, 0, bl)
    full, part = live == bl, (live > 0) & (live < bl)
    before = jnp.sum((full[None, :] & (i[None, :] < i[:, None])).astype(jnp.int32), axis=1)
    n_full = jnp.sum(full.astype(jnp.int32))
    place = jnp.where(full, before, jnp.where(part, n_full, n))
    order = jnp.sum(jnp.where(place[None, :] == i[:, None], code[None, :], 0), axis=1)
    blocks = n_full + jnp.sum(part.astype(jnp.int32))
    return jnp.concatenate([order, jnp.stack([blocks, jnp.sum(live), info[0, 2 * per + 1]])])


def gather_kernel(*refs, takes, paged):
    dest, ids, pool_ref = refs[:3]
    out_ref, sem = refs[-2:]
    n = out_ref.shape[0]

    def one(i, carry):
        for at, (which, k) in enumerate(takes):
            pltpu.make_async_copy(
                pool_ref.at[ids[dest[which, i], k]], out_ref.at[i, pl.ds(2 * at, 2)], sem.at[0]
            ).start()
        return carry

    lax.fori_loop(0, n, one, 0)
    if paged:
        near, away = refs[3:5]
        half = near.shape[1]
        for i in range(n):
            out_ref[i, 2 * len(takes), :half] = near[i]
            out_ref[i, 2 * len(takes), half:] = away[i]
    filled = out_ref.at[:, pl.ds(0, 2 * len(takes))]
    pltpu.make_async_copy(filled, filled, sem.at[0]).wait()


def gather_blocks(dest, ids, pool, takes, pages=()):
    n = dest.shape[1]
    _, two, bl, _ = pool.shape
    rows = two * len(takes) + (1 if pages else 0)
    return pl.pallas_call(
        functools.partial(gather_kernel, takes=takes, paged=bool(pages)),
        out_shape=jax.ShapeDtypeStruct((n, rows, bl, HD), pool.dtype),
        in_specs=[SM, SM, ANY] + [VM] * len(pages),
        out_specs=VM,
        scratch_shapes=[pltpu.SemaphoreType.DMA((1,))],
        compiler_params=PARAMS,
        cost_estimate=pl.CostEstimate(flops=0, bytes_accessed=4 * n * rows * bl * HD, transcendentals=0),
    )(dest, ids, pool, *pages)


def lanes(x, times):
    return x if times == 1 else jnp.concatenate([x] * times, axis=1)


def scores(q_ref, g, k):
    return lax.dot_general(
        q_ref[:, g * HD : (g + 1) * HD], k, (((1,), (1,)), ((), ())), preferred_element_type=jnp.float32
    )


def add_keys(q_ref, k, v, ok, acc, m_s, l_s):
    heads = acc.shape[0]
    width = k.shape[0] // HD
    ahead = scores(q_ref, 0, k)
    for g in range(heads):
        s = ahead
        if g + 1 < heads:
            ahead = scores(q_ref, g + 1, k)
        if ok is not None:
            s = jnp.where(ok, s, NEG)
        m_prev = m_s[g]
        m = jnp.maximum(m_prev, jnp.max(s, axis=1, keepdims=True))
        p = jnp.exp2((s - lanes(m, width)) * RATE)
        if ok is not None:
            p = jnp.where(ok, p, 0.0)
        fade = jnp.exp2((m_prev - m) * RATE)
        m_s[g] = m
        part = p[:, :HD]
        for i in range(1, width):
            part = part + p[:, i * HD : (i + 1) * HD]
        l_s[g] = fade * l_s[g] + part
        mixed = jnp.dot(p.astype(jnp.bfloat16), v, preferred_element_type=jnp.float32)
        acc[g] = fade * acc[g] + mixed


def add_prefix(tab, q_ref, kv_hbm, kv, acc, m_s, l_s, sems, first):
    n, _, bl, _ = kv.shape
    per = min(CK // bl, n)
    ck = per * bl
    blocks, keys = tab[n], tab[n + 1]
    chunks = (blocks + per - 1) // per

    def load(ci):
        def one(i, carry):
            at = ci * per + i
            code = tab[at]
            pltpu.make_async_copy(
                kv_hbm.at[code // 16, pl.ds(2 * (first + code % 16), 2)], kv.at[at], sems.at[ci]
            ).start()
            return carry

        lax.fori_loop(0, per, one, 0)

    @pl.when(chunks > 0)
    def _():
        load(0)

    def one_chunk(ci, carry):
        @pl.when(ci + 1 < chunks)
        def _():
            load(ci + 1)

        at = pl.ds(ci * per, per)
        pltpu.make_async_copy(kv.at[at], kv.at[at], sems.at[ci]).wait()
        whole = keys >= (ci + 1) * ck

        def both():
            return kv[at, 0].reshape(ck, HD), kv[at, 1].reshape(ck, HD)

        @pl.when(whole)
        def _():
            add_keys(q_ref, *both(), None, acc, m_s, l_s)

        @pl.when(jnp.logical_not(whole))
        def _():
            ok = lax.broadcasted_iota(jnp.int32, (q_ref.shape[0], ck), 1) < keys - ci * ck
            add_keys(q_ref, *both(), ok, acc, m_s, l_s)

        return carry

    lax.fori_loop(0, chunks, one_chunk, 0)


def reset(acc, m_s, l_s):
    acc[...] = jnp.zeros_like(acc)
    l_s[...] = jnp.zeros_like(l_s)
    m_s[...] = jnp.full_like(m_s, NEG)


def write_part(o_ref, st_ref, acc, m_s, l_s):
    heads = acc.shape[0]
    lane = lax.broadcasted_iota(jnp.int32, m_s.shape[1:], 1)
    st = jnp.zeros(m_s.shape[1:], jnp.float32)
    for g in range(heads):
        total = jnp.sum(l_s[g], axis=1, keepdims=True)
        inverse = 1.0 / jnp.where(total > 0, total, 1.0)
        o_ref[:, g * HD : (g + 1) * HD] = (acc[g] * inverse).astype(o_ref.dtype)
        st = jnp.where(lane == g, m_s[g], st)
        st = jnp.where(lane == heads + g, total, st)
    st_ref[...] = st.T[: 2 * heads]


def partner_kernel(tab, q_ref, kv_hbm, o_ref, st_ref, kv, acc, m_s, l_s, sems, *, first):
    reset(acc, m_s, l_s)
    add_prefix(tab, q_ref, kv_hbm, kv, acc, m_s, l_s, sems, first)
    write_part(o_ref, st_ref, acc, m_s, l_s)


def causal_kernel(q_ref, k_ref, v_ref, o_ref, st_ref, acc, m_s, l_s):
    reset(acc, m_s, l_s)
    tokens = q_ref.shape[0]
    ok = lax.broadcasted_iota(jnp.int32, (tokens, tokens), 1) <= lax.broadcasted_iota(
        jnp.int32, (tokens, tokens), 0
    )
    add_keys(q_ref, k_ref[...], v_ref[...], ok, acc, m_s, l_s)
    write_part(o_ref, st_ref, acc, m_s, l_s)


def late_kernel(
    tab, q_ref, kv_hbm, oa, sa, ob, sb, rows, keep_ref, give_ref, kv, acc, m_s, l_s, sems, out, *, first
):
    reset(acc, m_s, l_s)
    add_prefix(tab, q_ref, kv_hbm, kv, acc, m_s, l_s, sems, first)
    heads, tokens, _ = acc.shape
    fill = jnp.zeros((HD - 2 * heads, tokens), jnp.float32)
    ta = jnp.concatenate([sa[...], fill], axis=0).T
    tb = jnp.concatenate([sb[...], fill], axis=0).T
    alive = lax.broadcasted_iota(jnp.int32, (tokens, HD), 0) < tab[kv.shape[0] + 2]
    for g in range(heads):
        cols = slice(g * HD, (g + 1) * HD)
        m_a, l_a = ta[:, g : g + 1], ta[:, heads + g : heads + g + 1]
        m_b, l_b = tb[:, g : g + 1], tb[:, heads + g : heads + g + 1]
        m_o = m_s[g][:, :1]
        l_o = jnp.sum(l_s[g], axis=1, keepdims=True)
        m = jnp.maximum(jnp.maximum(m_o, m_a), m_b)
        w_o = jnp.exp2((m_o - m) * RATE)
        w_a = l_a * jnp.exp2((m_a - m) * RATE)
        w_b = l_b * jnp.exp2((m_b - m) * RATE)
        inverse = 1.0 / (l_o * w_o + w_a + w_b)
        mixed = (
            acc[g] * (w_o * inverse)
            + oa[:, cols].astype(jnp.float32) * (w_a * inverse)
            + ob[:, cols] * (w_b * inverse)
        )
        out[:, cols] = jnp.where(alive, mixed, 0.0).astype(out.dtype)
    chunk = keep_ref.shape[0] // NL
    for i in range(NL):
        at = pl.ds(i * chunk, chunk)
        keep_ref[at] = out[pl.ds(pl.multiple_of(rows[i] * chunk, chunk), chunk)]
        give_ref[at] = out[pl.ds(pl.multiple_of(rows[NL + i] * chunk, chunk), chunk)]


def state_of(heads, tokens):
    return [pltpu.VMEM((heads, tokens, HD), jnp.float32)] * 3


def causal_attention(q, k, v, out_types):
    tokens, width = q.shape
    return pl.pallas_call(
        causal_kernel,
        out_shape=out_types,
        in_specs=[VM] * 3,
        out_specs=[VM] * 2,
        scratch_shapes=state_of(width // HD, tokens),
        compiler_params=PARAMS,
        cost_estimate=pl.CostEstimate(
            flops=4 * tokens * width * tokens, bytes_accessed=8 * tokens * width, transcendentals=tokens * tokens * 4
        ),
    )(q, k, v)


def attention(body, tab, q, kv, more, more_specs, out_types, first, more_scratch=()):
    n, bl = tab.shape[0] - 3, kv.shape[2]
    tokens, width = q.shape
    heads = width // HD
    keys = n * bl
    return pl.pallas_call(
        functools.partial(body, first=first),
        out_shape=out_types,
        in_specs=[SM, VM, ANY] + more_specs,
        out_specs=[VM] * len(out_types),
        scratch_shapes=[
            pltpu.VMEM((n, 2, bl, HD), jnp.bfloat16),
            *state_of(heads, tokens),
            pltpu.SemaphoreType.DMA((max(keys // CK, 1),)),
            *more_scratch,
        ],
        compiler_params=PARAMS,
        cost_estimate=pl.CostEstimate(
            flops=4 * tokens * width * keys, bytes_accessed=keys * HD * 4, transcendentals=tokens * heads * keys
        ),
    )(tab, q, kv, *more)


def project_kernel(x_a, x_b, w_a, w_b, *outs):
    part = jnp.dot(x_a[...], w_a[...], preferred_element_type=jnp.float32)
    part = part + jnp.dot(x_b[...], w_b[...], preferred_element_type=jnp.float32)
    chunk = outs[0].shape[0]
    for i, out in enumerate(outs):
        out[...] = part[i * chunk : (i + 1) * chunk].astype(out.dtype)


def project(x_a, x_b, w_a, w_b, cols=512):
    rows, depth = x_a.shape
    width = w_a.shape[1]
    whole = pl.BlockSpec((rows, depth), lambda c: (0, 0))
    tall = pl.BlockSpec((depth, cols), lambda c: (0, c))
    return pl.pallas_call(
        project_kernel,
        grid=(width // cols,),
        out_shape=[jax.ShapeDtypeStruct((rows // NL, width), x_a.dtype)] * NL,
        in_specs=[whole, whole, tall, tall],
        out_specs=[pl.BlockSpec((rows // NL, cols), lambda c: (0, c))] * NL,
        compiler_params=PARAMS,
        cost_estimate=pl.CostEstimate(
            flops=4 * rows * depth * width, bytes_accessed=4 * depth * width + 2 * rows * width, transcendentals=0
        ),
    )(x_a, x_b, w_a, w_b)


def along_z(hops):
    return [(2 * a + k, 2 * b + k) for a, b in hops for k in range(2)]


def scatter_sum(own, for_b, for_ac, for_d):
    f32 = jnp.float32
    from_a = lax.ppermute(for_ac, "tp", along_z([(0, 1), (3, 2)]))
    from_b = lax.ppermute(for_b, "tp", along_z([(0, 2), (3, 1), (1, 0), (2, 3)]))
    from_c = lax.ppermute(for_ac, "tp", along_z([(1, 2), (2, 1)]))
    for_d = (for_d.astype(f32) + from_a.astype(f32)).astype(own.dtype)
    from_d = lax.ppermute(for_d, "tp", along_z([(0, 1), (1, 3), (3, 2), (2, 0)]))
    summed = own.astype(f32) + from_b.astype(f32) + from_c.astype(f32) + from_d.astype(f32)
    return summed.astype(own.dtype)


def local(
    queries,
    new_keys,
    new_values,
    kv_pool,
    out_weight,
    prefix_len,
    new_count,
    hit_holder,
    hit_block,
    decode_owner,
):
    n_pool = lax.axis_size("pool")
    per = hit_holder.shape[1] // n_pool
    tokens, width = queries.shape
    heads = width // HD
    bl = kv_pool.shape[2]
    plane_n = NX * NY
    me = lax.axis_index("pool")
    t_me = lax.axis_index("tp")
    zh = (me // NY) % NZ
    flip = [(p, p ^ NY) for p in range(n_pool)]
    cores = [(t, t ^ 1) for t in range(2 * NL)]
    planes = [[(x * NZ + z) * NY + y for x in range(NX) for y in range(NY)] for z in range(NZ)]

    def a2a(x, groups=None):
        return lax.all_to_all(x, "pool", 0, 0, axis_index_groups=groups, tiled=True)

    info = plan(hit_holder, hit_block, prefix_len, new_count, n_pool)
    ids = a2a(info)
    q_far = lax.ppermute(queries, "pool", flip)
    info_far = lax.ppermute(info, "pool", flip)
    w_other = lax.ppermute(out_weight, "tp", cores)

    i = jnp.arange(plane_n, dtype=jnp.int32)
    base = (i // NY) * (NZ * NY) + i % NY
    dest = jnp.stack([base + zh * NY, base + (1 - zh) * NY])
    send_a = gather_blocks(dest, ids, kv_pool, [(1, k) for k in range(per)])
    got_a = a2a(send_a, planes)

    _, owner, count, k_new, v_new, info_far, info = lax.optimization_barrier(
        (send_a, decode_owner[0], new_count, new_keys, new_values, info_far, info)
    )
    keep = (jnp.arange(tokens, dtype=jnp.int32) < count[0])[:, None]
    both = jnp.stack([jnp.where(keep, k_new, 0), jnp.where(keep, v_new, 0)])
    pages = owner.shape[0]
    both = both.reshape(2, pages, PG, HD)
    i = jnp.arange(pages, dtype=jnp.int32)
    page_of = jnp.sum(jnp.where(owner[None, :] == i[:, None], i[None, :], 0), axis=1)
    ordered = jnp.transpose(both[:, page_of], (1, 0, 2, 3)).reshape(NX, NZ, NY, 2 * PG, HD)
    near = lax.dynamic_index_in_dim(ordered, zh, 1, keepdims=False).reshape(plane_n, 2 * PG, HD)
    away = lax.dynamic_index_in_dim(ordered, 1 - zh, 1, keepdims=False).reshape(plane_n, 2 * PG, HD)
    away = lax.ppermute(away, "pool", flip)

    send_b = gather_blocks(dest, ids, kv_pool, [(0, k) for k in range(per)], (near, away))
    tab_far = block_table(info_far, zh, per, (0, per), bl)
    tab = block_table(info, zh, per, (0, per), bl)
    st_type = jax.ShapeDtypeStruct((2 * heads, tokens), jnp.float32)
    o_type = jax.ShapeDtypeStruct((tokens, width), jnp.bfloat16)
    o_wide = jax.ShapeDtypeStruct((tokens, width), jnp.float32)
    o_b, st_b = causal_attention(queries, k_new, v_new, [o_wide, st_type])
    send_b, q_far, w_other, tab_far, tab, o_b, st_b = lax.optimization_barrier(
        (send_b, q_far, w_other, tab_far, tab, o_b, st_b)
    )
    got_b = a2a(send_b, planes)

    o_far, st_far = attention(partner_kernel, tab_far, q_far, got_a, (), [], [o_type, st_type], 0)
    o_a = lax.ppermute(o_far, "pool", flip)
    st_a = lax.ppermute(st_far, "pool", flip)

    core, j = t_me % 2, t_me // 2
    mine = 2 * jnp.array(SENDS, jnp.int32)[j]
    rows = jnp.concatenate([mine + core, mine + 1 - core])
    half = jax.ShapeDtypeStruct((tokens // 2, width), jnp.bfloat16)
    x_keep, x_give = attention(
        late_kernel, tab, queries, got_b, (o_a, st_a, o_b, st_b, rows), [VM] * 4 + [SM], [half, half], 0,
        (pltpu.VMEM((tokens, width), jnp.bfloat16),),
    )
    x_got = lax.ppermute(x_give, "tp", cores)
    summed = scatter_sum(*project(x_keep, x_got, out_weight, w_other))

    arrived = got_b[:, 2 * per].reshape(NX, NY, 2, 2 * PG, HD)
    near_in, far_in = arrived[:, :, 0], arrived[:, :, 1]
    by_z = jnp.where(zh == 0, jnp.stack([near_in, far_in], 1), jnp.stack([far_in, near_in], 1))
    decode = by_z.reshape(n_pool, 1, 2, PG, HD)[None]
    return (summed, decode)


def solution(mesh):
    in_specs = (
        P("pool", "tp"),
        P("pool", "tp"),
        P("pool", "tp"),
        P("pool", None, None, "tp"),
        P("tp", None),
        P("pool"),
        P("pool"),
        P("pool", None),
        P("pool", None),
        P("pool", None),
    )
    out_specs = (P(("pool", "tp"), None), P("pool", None, None, None, None, "tp"))
    return jax.shard_map(local, mesh=mesh, in_specs=in_specs, out_specs=out_specs, check_vma=False)
```

```python
import functools

import jax
import jax.numpy as jnp
from jax import lax
from jax.experimental import pallas as pl
from jax.experimental.pallas import tpu as pltpu
from jax.sharding import PartitionSpec as P

HD = 128
PG = 16
NX, NZ, NY = 4, 2, 4
NL = 4
SENDS = ((0, 2, 3, 1), (1, 0, 2, 3), (2, 3, 1, 0), (3, 1, 0, 2))
CK = 1024
NEG = -1e30
RATE = HD ** (-0.5) * 1.4426950408889634

VM = pl.BlockSpec(memory_space=pltpu.VMEM)
SM = pl.BlockSpec(memory_space=pltpu.SMEM)
ANY = pl.BlockSpec(memory_space=pl.ANY)
LARGE = pltpu.CompilerParams(vmem_limit_bytes=62 * 1024 * 1024)
SMALL = pltpu.CompilerParams(vmem_limit_bytes=24 * 1024 * 1024)


def plan_kernel(holder, block, prefix_len, new_count, out):
    n = out.shape[0]
    slots = holder.shape[1]
    per = slots // n
    hit = lax.broadcasted_iota(jnp.int32, (n, slots), 0) == holder[...]
    lane = lax.broadcasted_iota(jnp.int32, (slots, slots), 1)
    earlier = (lax.broadcasted_iota(jnp.int32, (slots, slots), 0) < lane).astype(jnp.float32)
    rank = jnp.dot(hit.astype(jnp.float32), earlier, preferred_element_type=jnp.float32)
    at = lax.broadcasted_iota(jnp.int32, (n, out.shape[1]), 1)
    spot = lax.broadcasted_iota(jnp.int32, (n, slots), 1)
    ids = jnp.broadcast_to(block[...], (n, slots))
    row = jnp.where(at == 2 * per, prefix_len[0], 0) + jnp.where(at == 2 * per + 1, new_count[0], 0)
    for k in range(per):
        one = hit & (rank == k)
        row = jnp.where(at == k, jnp.sum(jnp.where(one, ids, 0), axis=1, keepdims=True), row)
        row = jnp.where(at == per + k, jnp.sum(jnp.where(one, spot, 0), axis=1, keepdims=True), row)
    out[...] = row


def plan(hit_holder, hit_block, prefix_len, new_count, n_pool):
    return pl.pallas_call(
        plan_kernel,
        out_shape=jax.ShapeDtypeStruct((n_pool, HD), jnp.int32),
        in_specs=[VM, VM, SM, SM],
        out_specs=VM,
        cost_estimate=pl.CostEstimate(flops=2 * n_pool * HD * HD, bytes_accessed=n_pool * HD * 4, transcendentals=0),
    )(hit_holder, hit_block, prefix_len, new_count)


def block_table(info, zh, per, ranks, bl):
    grid = info[:, per : 2 * per].reshape(NX, NZ, NY, per)
    pos = lax.dynamic_index_in_dim(grid, zh, 1, keepdims=False).reshape(NX * NY, per)
    pos = pos[:, ranks[0] : ranks[1]].reshape(-1)
    n = pos.shape[0]
    i = jnp.arange(n, dtype=jnp.int32)
    code = (i // (ranks[1] - ranks[0])) * 16 + i % (ranks[1] - ranks[0])
    live = jnp.clip(info[0, 2 * per] - pos * bl, 0, bl)
    full, part = live == bl, (live > 0) & (live < bl)
    before = jnp.sum((full[None, :] & (i[None, :] < i[:, None])).astype(jnp.int32), axis=1)
    n_full = jnp.sum(full.astype(jnp.int32))
    place = jnp.where(full, before, jnp.where(part, n_full, n))
    order = jnp.sum(jnp.where(place[None, :] == i[:, None], code[None, :], 0), axis=1)
    blocks = n_full + jnp.sum(part.astype(jnp.int32))
    return jnp.concatenate([order, jnp.stack([blocks, jnp.sum(live), info[0, 2 * per + 1]])])


def gather_kernel(*refs, takes, paged):
    dest, ids, pool_ref = refs[:3]
    out_ref, sem = refs[-2:]
    n = out_ref.shape[0]

    def one(i, carry):
        for at, (which, k) in enumerate(takes):
            pltpu.make_async_copy(
                pool_ref.at[ids[dest[which, i], k]], out_ref.at[i, pl.ds(2 * at, 2)], sem.at[0]
            ).start()
        return carry

    lax.fori_loop(0, n, one, 0)
    if paged:
        near, away = refs[3:5]
        half = near.shape[1]
        for i in range(n):
            out_ref[i, 2 * len(takes), :half] = near[i]
            out_ref[i, 2 * len(takes), half:] = away[i]
    filled = out_ref.at[:, pl.ds(0, 2 * len(takes))]
    pltpu.make_async_copy(filled, filled, sem.at[0]).wait()


def gather_blocks(dest, ids, pool, takes, pages=()):
    n = dest.shape[1]
    _, two, bl, _ = pool.shape
    rows = two * len(takes) + (1 if pages else 0)
    return pl.pallas_call(
        functools.partial(gather_kernel, takes=takes, paged=bool(pages)),
        out_shape=jax.ShapeDtypeStruct((n, rows, bl, HD), pool.dtype),
        in_specs=[SM, SM, ANY] + [VM] * len(pages),
        out_specs=VM,
        scratch_shapes=[pltpu.SemaphoreType.DMA((1,))],
        compiler_params=LARGE,
        cost_estimate=pl.CostEstimate(flops=0, bytes_accessed=4 * n * rows * bl * HD, transcendentals=0),
    )(dest, ids, pool, *pages)


def lanes(x, times):
    return x if times == 1 else jnp.concatenate([x] * times, axis=1)


def scores(q_ref, g, k):
    return lax.dot_general(
        q_ref[:, g * HD : (g + 1) * HD], k, (((1,), (1,)), ((), ())), preferred_element_type=jnp.float32
    )


def add_keys(q_ref, k, v, ok, acc, m_s, l_s):
    heads = acc.shape[0]
    width = k.shape[0] // HD
    ahead = scores(q_ref, 0, k)
    for g in range(heads):
        s = ahead
        if g + 1 < heads:
            ahead = scores(q_ref, g + 1, k)
        if ok is not None:
            s = jnp.where(ok, s, NEG)
        m_prev = m_s[g]
        m = jnp.maximum(m_prev, jnp.max(s, axis=1, keepdims=True))
        p = jnp.exp2((s - lanes(m, width)) * RATE)
        if ok is not None:
            p = jnp.where(ok, p, 0.0)
        fade = jnp.exp2((m_prev - m) * RATE)
        m_s[g] = m
        part = p[:, :HD]
        for i in range(1, width):
            part = part + p[:, i * HD : (i + 1) * HD]
        l_s[g] = fade * l_s[g] + part
        mixed = jnp.dot(p.astype(jnp.bfloat16), v, preferred_element_type=jnp.float32)
        acc[g] = fade * acc[g] + mixed


def load_chunk(tab, kv_in, kv, sems, ci):
    n, _, bl, _ = kv.shape
    per = min(CK // bl, n)

    def one(i, carry):
        at = ci * per + i
        code = tab[at]
        pltpu.make_async_copy(
            kv_in.at[code // 16, pl.ds(2 * (code % 16), 2)], kv.at[at], sems.at[ci]
        ).start()
        return carry

    @pl.when(ci * per < tab[n])
    def _():
        lax.fori_loop(0, per, one, 0)


def add_prefix(tab, q_ref, kv_in, kv, acc, m_s, l_s, sems):
    n, _, bl, _ = kv.shape
    per = min(CK // bl, n)
    ck = per * bl
    blocks, keys = tab[n], tab[n + 1]
    chunks = (blocks + per - 1) // per

    def one_chunk(ci, carry):
        load_chunk(tab, kv_in, kv, sems, ci + 1)
        at = pl.ds(ci * per, per)
        pltpu.make_async_copy(kv.at[at], kv.at[at], sems.at[ci]).wait()
        whole = keys >= (ci + 1) * ck

        def both():
            return kv[at, 0].reshape(ck, HD), kv[at, 1].reshape(ck, HD)

        @pl.when(whole)
        def _():
            add_keys(q_ref, *both(), None, acc, m_s, l_s)

        @pl.when(jnp.logical_not(whole))
        def _():
            ok = lax.broadcasted_iota(jnp.int32, (q_ref.shape[0], ck), 1) < keys - ci * ck
            add_keys(q_ref, *both(), ok, acc, m_s, l_s)

        return carry

    lax.fori_loop(0, chunks, one_chunk, 0)


def reset(acc, m_s, l_s):
    acc[...] = jnp.zeros_like(acc)
    l_s[...] = jnp.zeros_like(l_s)
    m_s[...] = jnp.full_like(m_s, NEG)


def write_part(o_ref, st_ref, acc, m_s, l_s):
    heads, tokens, _ = acc.shape
    lane = lax.broadcasted_iota(jnp.int32, (tokens, HD), 1)
    st = jnp.zeros((tokens, HD), jnp.float32)
    for g in range(heads):
        total = jnp.sum(l_s[g], axis=1, keepdims=True)
        inverse = 1.0 / jnp.where(total > 0, total, 1.0)
        o_ref[:, g * HD : (g + 1) * HD] = (acc[g] * inverse).astype(o_ref.dtype)
        st = jnp.where(lane == g, m_s[g], st)
        st = jnp.where(lane == heads + g, total, st)
    st_ref[...] = st.T[: 2 * heads] if st_ref.shape[0] == 2 * heads else st


def begin(tab, q_in, kv_in, q, kv, acc, m_s, l_s, sems):
    copy = pltpu.make_async_copy(q_in, q, sems.at[sems.shape[0] - 1])
    copy.start()
    load_chunk(tab, kv_in, kv, sems, 0)
    reset(acc, m_s, l_s)
    copy.wait()


def partner_kernel(tab, q_in, kv_in, o_ref, st_ref, q, kv, acc, m_s, l_s, sems):
    begin(tab, q_in, kv_in, q, kv, acc, m_s, l_s, sems)
    add_prefix(tab, q, kv_in, kv, acc, m_s, l_s, sems)
    write_part(o_ref, st_ref, acc, m_s, l_s)


def own_kernel(tab, q_in, kv_in, k_ref, v_ref, o_ref, st_ref, q, kv, acc, m_s, l_s, sems):
    begin(tab, q_in, kv_in, q, kv, acc, m_s, l_s, sems)
    tokens = q.shape[0]
    ok = lax.broadcasted_iota(jnp.int32, (tokens, tokens), 1) <= lax.broadcasted_iota(
        jnp.int32, (tokens, tokens), 0
    )
    add_keys(q, k_ref[...], v_ref[...], ok, acc, m_s, l_s)
    add_prefix(tab, q, kv_in, kv, acc, m_s, l_s, sems)
    write_part(o_ref, st_ref, acc, m_s, l_s)


def fold(parts, g, heads):
    m = functools.reduce(jnp.maximum, [m_i for _, m_i, _ in parts])
    shares = [l_i * jnp.exp2((m_i - m) * RATE) for _, m_i, l_i in parts]
    total = functools.reduce(jnp.add, shares)
    inverse = 1.0 / total
    mixed = functools.reduce(jnp.add, [o_i * (w * inverse) for (o_i, _, _), w in zip(parts, shares)])
    return mixed, m, total


def columns(st_ref):
    rows, tokens = st_ref.shape
    return jnp.concatenate([st_ref[...], jnp.zeros((HD - rows, tokens), jnp.float32)], axis=0).T


def stored(o_ref, st, g, heads):
    return (
        o_ref[:, g * HD : (g + 1) * HD].astype(jnp.float32),
        st[:, g : g + 1],
        st[:, heads + g : heads + g + 1],
    )


def merge_kernel(rows, count, oa, sa, ob, sb, *refs):
    outs, out = refs[:-1], refs[-1]
    tokens, width = oa.shape
    heads = width // HD
    ta, tb = columns(sa), sb[...]
    alive = lax.broadcasted_iota(jnp.int32, (tokens, HD), 0) < count[0]
    for g in range(heads):
        mixed, _, _ = fold([stored(oa, ta, g, heads), stored(ob, tb, g, heads)], g, heads)
        out[:, g * HD : (g + 1) * HD] = jnp.where(alive, mixed, 0.0).astype(out.dtype)
    chunk = tokens // (2 * NL)
    per = outs[0].shape[0] // chunk
    for i, o_ref in enumerate(outs):
        for k in range(per):
            o_ref[k * chunk : (k + 1) * chunk] = out[pl.ds(pl.multiple_of(rows[i * per + k] * chunk, chunk), chunk)]


def merge(rows, count, oa, sa, ob, sb):
    tokens, width = oa.shape
    half = jax.ShapeDtypeStruct((tokens // 2, width), jnp.bfloat16)
    return pl.pallas_call(
        merge_kernel,
        out_shape=[half] * 2,
        in_specs=[SM, SM] + [VM] * 4,
        out_specs=[VM] * 2,
        scratch_shapes=[pltpu.VMEM((tokens, width), jnp.bfloat16)],
        compiler_params=SMALL,
        cost_estimate=pl.CostEstimate(flops=8 * tokens * width, bytes_accessed=10 * tokens * width, transcendentals=0),
    )(rows, count, oa, sa, ob, sb)


def state_of(heads, tokens):
    return [pltpu.VMEM((heads, tokens, HD), jnp.float32)] * 3


def attention(body, tab, q, kv, more, more_specs, out_types, params):
    n, bl = tab.shape[0] - 3, kv.shape[2]
    tokens, width = q.shape
    heads = width // HD
    keys = n * bl
    return pl.pallas_call(
        body,
        out_shape=out_types,
        in_specs=[SM, ANY, ANY] + more_specs,
        out_specs=[VM] * len(out_types),
        scratch_shapes=[
            pltpu.VMEM((tokens, width), jnp.bfloat16),
            pltpu.VMEM((n, 2, bl, HD), jnp.bfloat16),
            *state_of(heads, tokens),
            pltpu.SemaphoreType.DMA((max(keys // CK, 1) + 1,)),
        ],
        compiler_params=params,
        cost_estimate=pl.CostEstimate(
            flops=4 * tokens * width * keys, bytes_accessed=keys * HD * 4, transcendentals=tokens * heads * keys
        ),
    )(tab, q, kv, *more)


def project_kernel(x_a, x_b, w_a, w_b, *refs):
    (*outs, buf, sems) = refs
    blocks, _, cols = buf.shape

    def copy(c):
        at = pl.ds(pl.multiple_of(c * cols, cols), cols)
        return pltpu.make_async_copy(w_b.at[:, at], buf.at[c], sems.at[c])

    def start(c, carry):
        copy(c).start()
        return carry

    lax.fori_loop(0, blocks, start, 0)

    def block(c, carry):
        at = pl.ds(pl.multiple_of(c * cols, cols), cols)
        part = jnp.dot(x_a[...], w_a[:, at], preferred_element_type=jnp.float32)
        copy(c).wait()
        part = part + jnp.dot(x_b[...], buf[c], preferred_element_type=jnp.float32)
        chunk = part.shape[0] // len(outs)
        for i, out in enumerate(outs):
            out[:, at] = part[i * chunk : (i + 1) * chunk].astype(out.dtype)
        return carry

    lax.fori_loop(0, blocks, block, 0)


def project(x_a, x_b, w_a, w_b, cols=1024):
    rows, depth = x_a.shape
    width = w_a.shape[1]
    return pl.pallas_call(
        project_kernel,
        out_shape=[jax.ShapeDtypeStruct((rows // NL, width), x_a.dtype)] * NL,
        in_specs=[VM, VM, VM, ANY],
        out_specs=[VM] * NL,
        scratch_shapes=[
            pltpu.VMEM((width // cols, depth, cols), w_b.dtype),
            pltpu.SemaphoreType.DMA((width // cols,)),
        ],
        compiler_params=SMALL,
        cost_estimate=pl.CostEstimate(
            flops=4 * rows * depth * width, bytes_accessed=4 * depth * width + 2 * rows * width, transcendentals=0
        ),
    )(x_a, x_b, w_a, w_b)


def along_z(hops):
    return [(2 * a + k, 2 * b + k) for a, b in hops for k in range(2)]


def scatter_start(own, for_b, for_ac, for_d):
    from_a = lax.ppermute(for_ac, "tp", along_z([(0, 1), (3, 2)]))
    from_b = lax.ppermute(for_b, "tp", along_z([(0, 2), (3, 1), (1, 0), (2, 3)]))
    from_c = lax.ppermute(for_ac, "tp", along_z([(1, 2), (2, 1)]))
    return [own, for_d, from_a, from_b, from_c]


def scatter_end(own, for_d, from_a, from_b, from_c):
    f32 = jnp.float32
    for_d = (for_d.astype(f32) + from_a.astype(f32)).astype(own.dtype)
    from_d = lax.ppermute(for_d, "tp", along_z([(0, 1), (1, 3), (3, 2), (2, 0)]))
    summed = own.astype(f32) + from_b.astype(f32) + from_c.astype(f32) + from_d.astype(f32)
    return summed.astype(own.dtype)


def local(
    queries,
    new_keys,
    new_values,
    kv_pool,
    out_weight,
    prefix_len,
    new_count,
    hit_holder,
    hit_block,
    decode_owner,
):
    n_pool = lax.axis_size("pool")
    per = hit_holder.shape[1] // n_pool
    tokens, width = queries.shape
    heads = width // HD
    bl = kv_pool.shape[2]
    plane_n = NX * NY
    me = lax.axis_index("pool")
    t_me = lax.axis_index("tp")
    zh = (me // NY) % NZ
    flip = [(p, p ^ NY) for p in range(n_pool)]
    planes = [[(x * NZ + z) * NY + y for x in range(NX) for y in range(NY)] for z in range(NZ)]

    def swap(x, bits):
        return lax.ppermute(x, "tp", [(t, t ^ bits) for t in range(2 * NL)])

    def a2a(x, groups=None):
        return lax.all_to_all(x, "pool", 0, 0, axis_index_groups=groups, tiled=True)

    info = plan(hit_holder, hit_block, prefix_len, new_count, n_pool)
    ids = a2a(info)
    q_far = lax.ppermute(queries, "pool", flip)
    info_far = lax.ppermute(info, "pool", flip)
    w_core = swap(out_weight, 1)
    info_far = lax.ppermute(info, "pool", flip)
    w_core = swap(out_weight, 1)
    x_y = (me // (NZ * NY)) * NY + me % NY
    piece = out_weight.shape[0] // plane_n
    w_piece = swap(lax.dynamic_slice_in_dim(out_weight, x_y * piece, piece, 0), 4)
    w_piece, ids = lax.optimization_barrier((w_piece, ids))
    w_z = lax.all_gather(w_piece, "pool", axis=0, tiled=True, axis_index_groups=planes)

    i = jnp.arange(plane_n, dtype=jnp.int32)
    base = (i // NY) * (NZ * NY) + i % NY
    dest = jnp.stack([base + zh * NY, base + (1 - zh) * NY])
    send_a = gather_blocks(dest, ids, kv_pool, [(1, k) for k in range(per)])
    got_a = a2a(send_a, planes)

    _, owner, count, k_new, v_new, info_far, info = lax.optimization_barrier(
        (send_a, decode_owner[0], new_count, new_keys, new_values, info_far, info)
    )
    keep = (jnp.arange(tokens, dtype=jnp.int32) < count[0])[:, None]
    both = jnp.stack([jnp.where(keep, k_new, 0), jnp.where(keep, v_new, 0)])
    pages = owner.shape[0]
    both = both.reshape(2, pages, PG, HD)
    i = jnp.arange(pages, dtype=jnp.int32)
    page_of = jnp.sum(jnp.where(owner[None, :] == i[:, None], i[None, :], 0), axis=1)
    ordered = jnp.transpose(both[:, page_of], (1, 0, 2, 3)).reshape(NX, NZ, NY, 2 * PG, HD)
    near = lax.dynamic_index_in_dim(ordered, zh, 1, keepdims=False).reshape(plane_n, 2 * PG, HD)
    away = lax.dynamic_index_in_dim(ordered, 1 - zh, 1, keepdims=False).reshape(plane_n, 2 * PG, HD)
    away = lax.ppermute(away, "pool", flip)

    send_b = gather_blocks(dest, ids, kv_pool, [(0, k) for k in range(per)], (near, away))
    tab_far = block_table(info_far, zh, per, (0, per), bl)
    tab = block_table(info, zh, per, (0, per), bl)
    send_b, q_far, w_core, tab_far, tab = lax.optimization_barrier((send_b, q_far, w_core, tab_far, tab))
    got_b = a2a(send_b, planes)

    st_type = jax.ShapeDtypeStruct((2 * heads, tokens), jnp.float32)
    st_wide = jax.ShapeDtypeStruct((tokens, HD), jnp.float32)
    o_type = jax.ShapeDtypeStruct((tokens, width), jnp.bfloat16)
    o_wide = jax.ShapeDtypeStruct((tokens, width), jnp.float32)
    o_a, st_a = attention(partner_kernel, tab_far, q_far, got_a, (), [], [o_type, st_type], LARGE)
    o_a, st_a = lax.ppermute(o_a, "pool", flip), lax.ppermute(st_a, "pool", flip)
    o_b, st_b = attention(own_kernel, tab, queries, got_b, (k_new, v_new), [VM] * 2, [o_wide, st_wide], SMALL)

    core, j = t_me % 2, t_me // 2
    mine = 2 * jnp.array(SENDS, jnp.int32)[j]
    rows = jnp.concatenate([mine + core, mine + 1 - core])
    x_keep, x_give = merge(rows, new_count, o_a, st_a, o_b, st_b)
    summed = scatter_end(*scatter_start(*project(x_keep, swap(x_give, 1), out_weight, w_core)))

    arrived = got_b[:, 2 * per].reshape(NX, NY, 2, 2 * PG, HD)
    near_in, far_in = arrived[:, :, 0], arrived[:, :, 1]
    by_z = jnp.where(zh == 0, jnp.stack([near_in, far_in], 1), jnp.stack([far_in, near_in], 1))
    decode = by_z.reshape(n_pool, 1, 2, PG, HD)[None]
    return (summed, decode)


def solution(mesh):
    in_specs = (
        P("pool", "tp"),
        P("pool", "tp"),
        P("pool", "tp"),
        P("pool", None, None, "tp"),
        P("tp", None),
        P("pool"),
        P("pool"),
        P("pool", None),
        P("pool", None),
        P("pool", None),
    )
    out_specs = (P(("pool", "tp"), None), P("pool", None, None, None, None, "tp"))
    return jax.shard_map(local, mesh=mesh, in_specs=in_specs, out_specs=out_specs, check_vma=False)
```

```python
import functools

import jax
import jax.numpy as jnp
from jax import lax
from jax.experimental import pallas as pl
from jax.experimental.pallas import tpu as pltpu
from jax.sharding import PartitionSpec as P

HD = 128
PG = 16
NX, NZ, NY = 4, 2, 4
NL = 4
SENDS = ((2, 3, 0, 1), (0, 2, 1, 3), (3, 1, 2, 0), (1, 0, 3, 2))
CK = 1024
NEG = -1e30
RATE = HD ** (-0.5) * 1.4426950408889634

VM = pl.BlockSpec(memory_space=pltpu.VMEM)
SM = pl.BlockSpec(memory_space=pltpu.SMEM)
ANY = pl.BlockSpec(memory_space=pl.ANY)
LARGE = pltpu.CompilerParams(vmem_limit_bytes=62 * 1024 * 1024)
SMALL = pltpu.CompilerParams(vmem_limit_bytes=24 * 1024 * 1024)


def plan_kernel(holder, block, prefix_len, new_count, out):
    n = out.shape[0]
    slots = holder.shape[1]
    per = slots // n
    hit = lax.broadcasted_iota(jnp.int32, (n, slots), 0) == holder[...]
    lane = lax.broadcasted_iota(jnp.int32, (slots, slots), 1)
    earlier = (lax.broadcasted_iota(jnp.int32, (slots, slots), 0) < lane).astype(jnp.float32)
    rank = jnp.dot(hit.astype(jnp.float32), earlier, preferred_element_type=jnp.float32)
    at = lax.broadcasted_iota(jnp.int32, (n, out.shape[1]), 1)
    spot = lax.broadcasted_iota(jnp.int32, (n, slots), 1)
    ids = jnp.broadcast_to(block[...], (n, slots))
    row = jnp.where(at == 2 * per, prefix_len[0], 0) + jnp.where(at == 2 * per + 1, new_count[0], 0)
    for k in range(per):
        one = hit & (rank == k)
        row = jnp.where(at == k, jnp.sum(jnp.where(one, ids, 0), axis=1, keepdims=True), row)
        row = jnp.where(at == per + k, jnp.sum(jnp.where(one, spot, 0), axis=1, keepdims=True), row)
    out[...] = row


def plan(hit_holder, hit_block, prefix_len, new_count, n_pool):
    return pl.pallas_call(
        plan_kernel,
        out_shape=jax.ShapeDtypeStruct((n_pool, HD), jnp.int32),
        in_specs=[VM, VM, SM, SM],
        out_specs=VM,
        cost_estimate=pl.CostEstimate(flops=2 * n_pool * HD * HD, bytes_accessed=n_pool * HD * 4, transcendentals=0),
    )(hit_holder, hit_block, prefix_len, new_count)


def block_table(info, zh, per, ranks, bl):
    grid = info[:, per : 2 * per].reshape(NX, NZ, NY, per)
    pos = lax.dynamic_index_in_dim(grid, zh, 1, keepdims=False).reshape(NX * NY, per)
    pos = pos[:, ranks[0] : ranks[1]].reshape(-1)
    n = pos.shape[0]
    i = jnp.arange(n, dtype=jnp.int32)
    code = (i // (ranks[1] - ranks[0])) * 16 + i % (ranks[1] - ranks[0])
    live = jnp.clip(info[0, 2 * per] - pos * bl, 0, bl)
    full, part = live == bl, (live > 0) & (live < bl)
    before = jnp.sum((full[None, :] & (i[None, :] < i[:, None])).astype(jnp.int32), axis=1)
    n_full = jnp.sum(full.astype(jnp.int32))
    place = jnp.where(full, before, jnp.where(part, n_full, n))
    order = jnp.sum(jnp.where(place[None, :] == i[:, None], code[None, :], 0), axis=1)
    blocks = n_full + jnp.sum(part.astype(jnp.int32))
    return jnp.concatenate([order, jnp.stack([blocks, jnp.sum(live), info[0, 2 * per + 1]])])


def gather_kernel(*refs, takes, paged):
    dest, ids, pool_ref = refs[:3]
    out_ref, sem = refs[-2:]
    n = out_ref.shape[0]

    def one(i, carry):
        for at, (which, k) in enumerate(takes):
            pltpu.make_async_copy(
                pool_ref.at[ids[dest[which, i], k]], out_ref.at[i, pl.ds(2 * at, 2)], sem.at[0]
            ).start()
        return carry

    lax.fori_loop(0, n, one, 0)
    if paged:
        near, away = refs[3:5]
        half = near.shape[1]
        for i in range(n):
            out_ref[i, 2 * len(takes), :half] = near[i]
            out_ref[i, 2 * len(takes), half:] = away[i]
    filled = out_ref.at[:, pl.ds(0, 2 * len(takes))]
    pltpu.make_async_copy(filled, filled, sem.at[0]).wait()


def gather_blocks(dest, ids, pool, takes, pages=()):
    n = dest.shape[1]
    _, two, bl, _ = pool.shape
    rows = two * len(takes) + (1 if pages else 0)
    return pl.pallas_call(
        functools.partial(gather_kernel, takes=takes, paged=bool(pages)),
        out_shape=jax.ShapeDtypeStruct((n, rows, bl, HD), pool.dtype),
        in_specs=[SM, SM, ANY] + [VM] * len(pages),
        out_specs=VM,
        scratch_shapes=[pltpu.SemaphoreType.DMA((1,))],
        compiler_params=LARGE,
        cost_estimate=pl.CostEstimate(flops=0, bytes_accessed=4 * n * rows * bl * HD, transcendentals=0),
    )(dest, ids, pool, *pages)


def lanes(x, times):
    return x if times == 1 else jnp.concatenate([x] * times, axis=1)


def scores(q_ref, g, k):
    return lax.dot_general(
        q_ref[:, g * HD : (g + 1) * HD], k, (((1,), (1,)), ((), ())), preferred_element_type=jnp.float32
    )


def add_keys(q_ref, k, v, ok, acc, m_s, l_s):
    heads = acc.shape[0]
    width = k.shape[0] // HD
    ahead = scores(q_ref, 0, k)
    for g in range(heads):
        s = ahead
        if g + 1 < heads:
            ahead = scores(q_ref, g + 1, k)
        if ok is not None:
            s = jnp.where(ok, s, NEG)
        m_prev = m_s[g]
        m = jnp.maximum(m_prev, jnp.max(s, axis=1, keepdims=True))
        p = jnp.exp2((s - lanes(m, width)) * RATE)
        if ok is not None:
            p = jnp.where(ok, p, 0.0)
        fade = jnp.exp2((m_prev - m) * RATE)
        m_s[g] = m
        part = p[:, :HD]
        for i in range(1, width):
            part = part + p[:, i * HD : (i + 1) * HD]
        l_s[g] = fade * l_s[g] + part
        mixed = jnp.dot(p.astype(jnp.bfloat16), v, preferred_element_type=jnp.float32)
        acc[g] = fade * acc[g] + mixed


def load_chunk(tab, kv_in, kv, sems, ci):
    n, _, bl, _ = kv.shape
    per = min(CK // bl, n)

    def one(i, carry):
        at = ci * per + i
        code = tab[at]
        pltpu.make_async_copy(
            kv_in.at[code // 16, pl.ds(2 * (code % 16), 2)], kv.at[at], sems.at[ci]
        ).start()
        return carry

    @pl.when(ci * per < tab[n])
    def _():
        lax.fori_loop(0, per, one, 0)


def add_prefix(tab, q_ref, kv_in, kv, acc, m_s, l_s, sems):
    n, _, bl, _ = kv.shape
    per = min(CK // bl, n)
    ck = per * bl
    blocks, keys = tab[n], tab[n + 1]
    chunks = (blocks + per - 1) // per

    def one_chunk(ci, carry):
        load_chunk(tab, kv_in, kv, sems, ci + 1)
        at = pl.ds(ci * per, per)
        pltpu.make_async_copy(kv.at[at], kv.at[at], sems.at[ci]).wait()
        whole = keys >= (ci + 1) * ck

        def both():
            return kv[at, 0].reshape(ck, HD), kv[at, 1].reshape(ck, HD)

        @pl.when(whole)
        def _():
            add_keys(q_ref, *both(), None, acc, m_s, l_s)

        @pl.when(jnp.logical_not(whole))
        def _():
            ok = lax.broadcasted_iota(jnp.int32, (q_ref.shape[0], ck), 1) < keys - ci * ck
            add_keys(q_ref, *both(), ok, acc, m_s, l_s)

        return carry

    lax.fori_loop(0, chunks, one_chunk, 0)


def reset(acc, m_s, l_s):
    acc[...] = jnp.zeros_like(acc)
    l_s[...] = jnp.zeros_like(l_s)
    m_s[...] = jnp.full_like(m_s, NEG)


def write_part(o_ref, st_ref, acc, m_s, l_s):
    heads, tokens, _ = acc.shape
    lane = lax.broadcasted_iota(jnp.int32, (tokens, HD), 1)
    st = jnp.zeros((tokens, HD), jnp.float32)
    for g in range(heads):
        total = jnp.sum(l_s[g], axis=1, keepdims=True)
        inverse = 1.0 / jnp.where(total > 0, total, 1.0)
        o_ref[:, g * HD : (g + 1) * HD] = (acc[g] * inverse).astype(o_ref.dtype)
        st = jnp.where(lane == g, m_s[g], st)
        st = jnp.where(lane == heads + g, total, st)
    st_ref[...] = st.T[: 2 * heads] if st_ref.shape[0] == 2 * heads else st


def begin(tab, q_in, kv_in, q, kv, acc, m_s, l_s, sems):
    copy = pltpu.make_async_copy(q_in, q, sems.at[sems.shape[0] - 1])
    copy.start()
    load_chunk(tab, kv_in, kv, sems, 0)
    reset(acc, m_s, l_s)
    copy.wait()


def partner_kernel(tab, q_in, kv_in, o_ref, st_ref, q, kv, acc, m_s, l_s, sems):
    begin(tab, q_in, kv_in, q, kv, acc, m_s, l_s, sems)
    add_prefix(tab, q, kv_in, kv, acc, m_s, l_s, sems)
    write_part(o_ref, st_ref, acc, m_s, l_s)


def own_kernel(tab, q_in, kv_in, k_ref, v_ref, o_ref, st_ref, q, kv, acc, m_s, l_s, sems):
    begin(tab, q_in, kv_in, q, kv, acc, m_s, l_s, sems)
    tokens = q.shape[0]
    ok = lax.broadcasted_iota(jnp.int32, (tokens, tokens), 1) <= lax.broadcasted_iota(
        jnp.int32, (tokens, tokens), 0
    )
    add_keys(q, k_ref[...], v_ref[...], ok, acc, m_s, l_s)
    add_prefix(tab, q, kv_in, kv, acc, m_s, l_s, sems)
    write_part(o_ref, st_ref, acc, m_s, l_s)


def fold(parts, g, heads):
    m = functools.reduce(jnp.maximum, [m_i for _, m_i, _ in parts])
    shares = [l_i * jnp.exp2((m_i - m) * RATE) for _, m_i, l_i in parts]
    total = functools.reduce(jnp.add, shares)
    inverse = 1.0 / total
    mixed = functools.reduce(jnp.add, [o_i * (w * inverse) for (o_i, _, _), w in zip(parts, shares)])
    return mixed, m, total


def columns(st_ref):
    rows, tokens = st_ref.shape
    return jnp.concatenate([st_ref[...], jnp.zeros((HD - rows, tokens), jnp.float32)], axis=0).T


def stored(o_ref, st, g, heads):
    return (
        o_ref[:, g * HD : (g + 1) * HD].astype(jnp.float32),
        st[:, g : g + 1],
        st[:, heads + g : heads + g + 1],
    )


def merge_kernel(rows, count, oa, sa, ob, sb, *refs):
    outs, out = refs[:-1], refs[-1]
    tokens, width = oa.shape
    heads = width // HD
    ta, tb = columns(sa), sb[...]
    alive = lax.broadcasted_iota(jnp.int32, (tokens, HD), 0) < count[0]
    for g in range(heads):
        mixed, _, _ = fold([stored(oa, ta, g, heads), stored(ob, tb, g, heads)], g, heads)
        out[:, g * HD : (g + 1) * HD] = jnp.where(alive, mixed, 0.0).astype(out.dtype)
    chunk = tokens // (2 * NL)
    per = outs[0].shape[0] // chunk
    for i, o_ref in enumerate(outs):
        for k in range(per):
            o_ref[k * chunk : (k + 1) * chunk] = out[pl.ds(pl.multiple_of(rows[i * per + k] * chunk, chunk), chunk)]


def merge(rows, count, oa, sa, ob, sb):
    tokens, width = oa.shape
    half = jax.ShapeDtypeStruct((tokens // 2, width), jnp.bfloat16)
    return pl.pallas_call(
        merge_kernel,
        out_shape=[half] * 2,
        in_specs=[SM, SM] + [VM] * 4,
        out_specs=[VM] * 2,
        scratch_shapes=[pltpu.VMEM((tokens, width), jnp.bfloat16)],
        compiler_params=SMALL,
        cost_estimate=pl.CostEstimate(flops=8 * tokens * width, bytes_accessed=10 * tokens * width, transcendentals=0),
    )(rows, count, oa, sa, ob, sb)


def state_of(heads, tokens):
    return [pltpu.VMEM((heads, tokens, HD), jnp.float32)] * 3


def attention(body, tab, q, kv, more, more_specs, out_types, params):
    n, bl = tab.shape[0] - 3, kv.shape[2]
    tokens, width = q.shape
    heads = width // HD
    keys = n * bl
    return pl.pallas_call(
        body,
        out_shape=out_types,
        in_specs=[SM, ANY, ANY] + more_specs,
        out_specs=[VM] * len(out_types),
        scratch_shapes=[
            pltpu.VMEM((tokens, width), jnp.bfloat16),
            pltpu.VMEM((n, 2, bl, HD), jnp.bfloat16),
            *state_of(heads, tokens),
            pltpu.SemaphoreType.DMA((max(keys // CK, 1) + 1,)),
        ],
        compiler_params=params,
        cost_estimate=pl.CostEstimate(
            flops=4 * tokens * width * keys, bytes_accessed=keys * HD * 4, transcendentals=tokens * heads * keys
        ),
    )(tab, q, kv, *more)


def project_kernel(x_a, x_b, w_a, w_b, *refs, first):
    (*outs, buf, sems) = refs
    blocks, _, cols = buf.shape

    def copy(c):
        at = pl.ds(pl.multiple_of(c * cols, cols), cols)
        return pltpu.make_async_copy(w_b.at[:, at], buf.at[c], sems.at[c])

    def start(c, carry):
        copy(c).start()
        return carry

    lax.fori_loop(0, blocks, start, 0)
    rows = pl.ds(first, len(outs) * outs[0].shape[0])

    def block(c, carry):
        at = pl.ds(pl.multiple_of(c * cols, cols), cols)
        part = jnp.dot(x_a[rows], w_a[:, at], preferred_element_type=jnp.float32)
        copy(c).wait()
        part = part + jnp.dot(x_b[rows], buf[c], preferred_element_type=jnp.float32)
        chunk = part.shape[0] // len(outs)
        for i, out in enumerate(outs):
            out[:, at] = part[i * chunk : (i + 1) * chunk].astype(out.dtype)
        return carry

    lax.fori_loop(0, blocks, block, 0)


def project(x_a, x_b, w_a, w_b, half, cols=1024):
    rows, depth = x_a.shape
    width = w_a.shape[1]
    return pl.pallas_call(
        functools.partial(project_kernel, first=half * (rows // 2)),
        out_shape=[jax.ShapeDtypeStruct((rows // NL, width), x_a.dtype)] * (NL // 2),
        in_specs=[VM, VM, VM, ANY],
        out_specs=[VM] * (NL // 2),
        scratch_shapes=[
            pltpu.VMEM((width // cols, depth, cols), w_b.dtype),
            pltpu.SemaphoreType.DMA((width // cols,)),
        ],
        compiler_params=SMALL,
        cost_estimate=pl.CostEstimate(
            flops=2 * rows * depth * width, bytes_accessed=4 * depth * width + 2 * rows * width, transcendentals=0
        ),
    )(x_a, x_b, w_a, w_b)


def along_z(hops):
    return [(2 * a + k, 2 * b + k) for a, b in hops for k in range(2)]


def scatter_start(own, for_b, for_ac, for_d):
    from_a = lax.ppermute(for_ac, "tp", along_z([(0, 1), (3, 2)]))
    from_b = lax.ppermute(for_b, "tp", along_z([(0, 2), (3, 1), (1, 0), (2, 3)]))
    from_c = lax.ppermute(for_ac, "tp", along_z([(1, 2), (2, 1)]))
    return [own, for_d, from_a, from_b, from_c]


def scatter_end(own, for_d, from_a, from_b, from_c):
    f32 = jnp.float32
    for_d = (for_d.astype(f32) + from_a.astype(f32)).astype(own.dtype)
    from_d = lax.ppermute(for_d, "tp", along_z([(0, 1), (1, 3), (3, 2), (2, 0)]))
    summed = own.astype(f32) + from_b.astype(f32) + from_c.astype(f32) + from_d.astype(f32)
    return summed.astype(own.dtype)


def local(
    queries,
    new_keys,
    new_values,
    kv_pool,
    out_weight,
    prefix_len,
    new_count,
    hit_holder,
    hit_block,
    decode_owner,
):
    n_pool = lax.axis_size("pool")
    per = hit_holder.shape[1] // n_pool
    tokens, width = queries.shape
    heads = width // HD
    bl = kv_pool.shape[2]
    plane_n = NX * NY
    me = lax.axis_index("pool")
    t_me = lax.axis_index("tp")
    zh = (me // NY) % NZ
    flip = [(p, p ^ NY) for p in range(n_pool)]
    planes = [[(x * NZ + z) * NY + y for x in range(NX) for y in range(NY)] for z in range(NZ)]

    def swap(x, bits):
        return lax.ppermute(x, "tp", [(t, t ^ bits) for t in range(2 * NL)])

    def a2a(x, groups=None):
        return lax.all_to_all(x, "pool", 0, 0, axis_index_groups=groups, tiled=True)

    info = plan(hit_holder, hit_block, prefix_len, new_count, n_pool)
    ids = a2a(info)
    q_far = lax.ppermute(queries, "pool", flip)
    info_far = lax.ppermute(info, "pool", flip)
    w_core = swap(out_weight, 1)
    info_far = lax.ppermute(info, "pool", flip)
    w_core = swap(out_weight, 1)
    x_y = (me // (NZ * NY)) * NY + me % NY
    piece = out_weight.shape[0] // plane_n
    w_piece = swap(lax.dynamic_slice_in_dim(out_weight, x_y * piece, piece, 0), 4)
    w_piece, ids = lax.optimization_barrier((w_piece, ids))
    w_z = lax.all_gather(w_piece, "pool", axis=0, tiled=True, axis_index_groups=planes)

    i = jnp.arange(plane_n, dtype=jnp.int32)
    base = (i // NY) * (NZ * NY) + i % NY
    dest = jnp.stack([base + zh * NY, base + (1 - zh) * NY])
    send_a = gather_blocks(dest, ids, kv_pool, [(1, k) for k in range(per)])
    got_a = a2a(send_a, planes)

    _, owner, count, k_new, v_new, info_far, info = lax.optimization_barrier(
        (send_a, decode_owner[0], new_count, new_keys, new_values, info_far, info)
    )
    keep = (jnp.arange(tokens, dtype=jnp.int32) < count[0])[:, None]
    both = jnp.stack([jnp.where(keep, k_new, 0), jnp.where(keep, v_new, 0)])
    pages = owner.shape[0]
    both = both.reshape(2, pages, PG, HD)
    i = jnp.arange(pages, dtype=jnp.int32)
    page_of = jnp.sum(jnp.where(owner[None, :] == i[:, None], i[None, :], 0), axis=1)
    ordered = jnp.transpose(both[:, page_of], (1, 0, 2, 3)).reshape(NX, NZ, NY, 2 * PG, HD)
    near = lax.dynamic_index_in_dim(ordered, zh, 1, keepdims=False).reshape(plane_n, 2 * PG, HD)
    away = lax.dynamic_index_in_dim(ordered, 1 - zh, 1, keepdims=False).reshape(plane_n, 2 * PG, HD)
    away = lax.ppermute(away, "pool", flip)

    send_b = gather_blocks(dest, ids, kv_pool, [(0, k) for k in range(per)], (near, away))
    tab_far = block_table(info_far, zh, per, (0, per), bl)
    tab = block_table(info, zh, per, (0, per), bl)
    send_b, q_far, w_core, tab_far, tab = lax.optimization_barrier((send_b, q_far, w_core, tab_far, tab))
    got_b = a2a(send_b, planes)

    st_type = jax.ShapeDtypeStruct((2 * heads, tokens), jnp.float32)
    st_wide = jax.ShapeDtypeStruct((tokens, HD), jnp.float32)
    o_type = jax.ShapeDtypeStruct((tokens, width), jnp.bfloat16)
    o_wide = jax.ShapeDtypeStruct((tokens, width), jnp.float32)
    o_a, st_a = attention(partner_kernel, tab_far, q_far, got_a, (), [], [o_type, st_type], LARGE)
    o_a, st_a = lax.ppermute(o_a, "pool", flip), lax.ppermute(st_a, "pool", flip)
    o_b, st_b = attention(own_kernel, tab, queries, got_b, (k_new, v_new), [VM] * 2, [o_wide, st_wide], SMALL)

    core, j = t_me % 2, t_me // 2
    mine = 2 * jnp.array(SENDS, jnp.int32)[j]
    rows = jnp.concatenate([mine + core, mine + 1 - core])
    x_keep, x_give = merge(rows, new_count, o_a, st_a, o_b, st_b)
    x = (x_keep, swap(x_give, 1), out_weight, w_core)
    for_b, for_ac = project(*x, 0)
    own, for_d = project(*x, 1)
    summed = scatter_end(*scatter_start(own, for_b, for_ac, for_d))

    arrived = got_b[:, 2 * per].reshape(NX, NY, 2, 2 * PG, HD)
    near_in, far_in = arrived[:, :, 0], arrived[:, :, 1]
    by_z = jnp.where(zh == 0, jnp.stack([near_in, far_in], 1), jnp.stack([far_in, near_in], 1))
    decode = by_z.reshape(n_pool, 1, 2, PG, HD)[None]
    return (summed, decode)


def solution(mesh):
    in_specs = (
        P("pool", "tp"),
        P("pool", "tp"),
        P("pool", "tp"),
        P("pool", None, None, "tp"),
        P("tp", None),
        P("pool"),
        P("pool"),
        P("pool", None),
        P("pool", None),
        P("pool", None),
    )
    out_specs = (P(("pool", "tp"), None), P("pool", None, None, None, None, "tp"))
    return jax.shard_map(local, mesh=mesh, in_specs=in_specs, out_specs=out_specs, check_vma=False)
```

```python
import functools

import jax
import jax.numpy as jnp
from jax import lax
from jax.experimental import pallas as pl
from jax.experimental.pallas import tpu as pltpu
from jax.sharding import PartitionSpec as P

HD = 128
PG = 16
NX, NZ, NY = 4, 2, 4
NL = 4
SENDS = ((2, 3, 0, 1), (0, 2, 1, 3), (3, 1, 2, 0), (1, 0, 3, 2))
CK = 1024
NEG = -1e30
RATE = HD ** (-0.5) * 1.4426950408889634

VM = pl.BlockSpec(memory_space=pltpu.VMEM)
SM = pl.BlockSpec(memory_space=pltpu.SMEM)
ANY = pl.BlockSpec(memory_space=pl.ANY)
LARGE = pltpu.CompilerParams(vmem_limit_bytes=62 * 1024 * 1024)
SMALL = pltpu.CompilerParams(vmem_limit_bytes=24 * 1024 * 1024)


def plan_kernel(holder, block, prefix_len, new_count, out):
    n = out.shape[0]
    slots = holder.shape[1]
    per = slots // n
    hit = lax.broadcasted_iota(jnp.int32, (n, slots), 0) == holder[...]
    lane = lax.broadcasted_iota(jnp.int32, (slots, slots), 1)
    earlier = (lax.broadcasted_iota(jnp.int32, (slots, slots), 0) < lane).astype(jnp.float32)
    rank = jnp.dot(hit.astype(jnp.float32), earlier, preferred_element_type=jnp.float32)
    at = lax.broadcasted_iota(jnp.int32, (n, out.shape[1]), 1)
    spot = lax.broadcasted_iota(jnp.int32, (n, slots), 1)
    ids = jnp.broadcast_to(block[...], (n, slots))
    row = jnp.where(at == 2 * per, prefix_len[0], 0) + jnp.where(at == 2 * per + 1, new_count[0], 0)
    for k in range(per):
        one = hit & (rank == k)
        row = jnp.where(at == k, jnp.sum(jnp.where(one, ids, 0), axis=1, keepdims=True), row)
        row = jnp.where(at == per + k, jnp.sum(jnp.where(one, spot, 0), axis=1, keepdims=True), row)
    out[...] = row


def plan(hit_holder, hit_block, prefix_len, new_count, n_pool):
    return pl.pallas_call(
        plan_kernel,
        out_shape=jax.ShapeDtypeStruct((n_pool, HD), jnp.int32),
        in_specs=[VM, VM, SM, SM],
        out_specs=VM,
        cost_estimate=pl.CostEstimate(flops=2 * n_pool * HD * HD, bytes_accessed=n_pool * HD * 4, transcendentals=0),
    )(hit_holder, hit_block, prefix_len, new_count)


def block_table(info, zh, per, ranks, bl):
    grid = info[:, per : 2 * per].reshape(NX, NZ, NY, per)
    pos = lax.dynamic_index_in_dim(grid, zh, 1, keepdims=False).reshape(NX * NY, per)
    pos = pos[:, ranks[0] : ranks[1]].reshape(-1)
    n = pos.shape[0]
    i = jnp.arange(n, dtype=jnp.int32)
    code = (i // (ranks[1] - ranks[0])) * 16 + i % (ranks[1] - ranks[0])
    live = jnp.clip(info[0, 2 * per] - pos * bl, 0, bl)
    full, part = live == bl, (live > 0) & (live < bl)
    before = jnp.sum((full[None, :] & (i[None, :] < i[:, None])).astype(jnp.int32), axis=1)
    n_full = jnp.sum(full.astype(jnp.int32))
    place = jnp.where(full, before, jnp.where(part, n_full, n))
    order = jnp.sum(jnp.where(place[None, :] == i[:, None], code[None, :], 0), axis=1)
    blocks = n_full + jnp.sum(part.astype(jnp.int32))
    return jnp.concatenate([order, jnp.stack([blocks, jnp.sum(live), info[0, 2 * per + 1]])])


def gather_kernel(*refs, takes, paged):
    dest, ids, pool_ref = refs[:3]
    out_ref, buf, sems = refs[-3:]
    n = out_ref.shape[0]
    groups = sems.shape[1]
    share = n // groups

    def one(i, carry):
        for at, (which, k) in enumerate(takes):
            pltpu.make_async_copy(
                pool_ref.at[ids[dest[which, i], k]], buf.at[i, pl.ds(2 * at, 2)], sems.at[0, i // share]
            ).start()
        return carry

    lax.fori_loop(0, n, one, 0)
    if paged:
        near, away = refs[3:5]
        half = near.shape[1]
        for i in range(n):
            buf[i, 2 * len(takes), :half] = near[i]
            buf[i, 2 * len(takes), half:] = away[i]
    for g in range(groups):
        rows = pl.ds(g * share, share)
        filled = buf.at[rows, pl.ds(0, 2 * len(takes))]
        pltpu.make_async_copy(filled, filled, sems.at[0, g]).wait()
        pltpu.make_async_copy(buf.at[rows], out_ref.at[rows], sems.at[1, g]).start()
    for g in range(groups):
        rows = pl.ds(g * share, share)
        pltpu.make_async_copy(buf.at[rows], out_ref.at[rows], sems.at[1, g]).wait()


def gather_blocks(dest, ids, pool, takes, pages=()):
    n = dest.shape[1]
    _, two, bl, _ = pool.shape
    rows = two * len(takes) + (1 if pages else 0)
    return pl.pallas_call(
        functools.partial(gather_kernel, takes=takes, paged=bool(pages)),
        out_shape=jax.ShapeDtypeStruct((n, rows, bl, HD), pool.dtype),
        in_specs=[SM, SM, ANY] + [VM] * len(pages),
        out_specs=ANY,
        scratch_shapes=[pltpu.VMEM((n, rows, bl, HD), pool.dtype), pltpu.SemaphoreType.DMA((2, 4))],
        compiler_params=LARGE,
        cost_estimate=pl.CostEstimate(flops=0, bytes_accessed=4 * n * rows * bl * HD, transcendentals=0),
    )(dest, ids, pool, *pages)


def lanes(x, times):
    return x if times == 1 else jnp.concatenate([x] * times, axis=1)


def scores(q_ref, g, k):
    return lax.dot_general(
        q_ref[:, g * HD : (g + 1) * HD], k, (((1,), (1,)), ((), ())), preferred_element_type=jnp.float32
    )


def add_keys(q_ref, k, v, ok, acc, m_s, l_s):
    heads = acc.shape[0]
    width = k.shape[0] // HD
    ahead = scores(q_ref, 0, k)
    for g in range(heads):
        s = ahead
        if g + 1 < heads:
            ahead = scores(q_ref, g + 1, k)
        if ok is not None:
            s = jnp.where(ok, s, NEG)
        m_prev = m_s[g]
        m = jnp.maximum(m_prev, jnp.max(s, axis=1, keepdims=True))
        p = jnp.exp2((s - lanes(m, width)) * RATE)
        if ok is not None:
            p = jnp.where(ok, p, 0.0)
        fade = jnp.exp2((m_prev - m) * RATE)
        m_s[g] = m
        part = p[:, :HD]
        for i in range(1, width):
            part = part + p[:, i * HD : (i + 1) * HD]
        l_s[g] = fade * l_s[g] + part
        mixed = jnp.dot(p.astype(jnp.bfloat16), v, preferred_element_type=jnp.float32)
        acc[g] = fade * acc[g] + mixed


def load_chunk(tab, kv_in, kv, sems, ci):
    n, _, bl, _ = kv.shape
    per = min(CK // bl, n)

    def one(i, carry):
        at = ci * per + i
        code = tab[at]
        pltpu.make_async_copy(
            kv_in.at[code // 16, pl.ds(2 * (code % 16), 2)], kv.at[at], sems.at[ci]
        ).start()
        return carry

    @pl.when(ci * per < tab[n])
    def _():
        lax.fori_loop(0, per, one, 0)


def add_prefix(tab, q_ref, kv_in, kv, acc, m_s, l_s, sems):
    n, _, bl, _ = kv.shape
    per = min(CK // bl, n)
    ck = per * bl
    blocks, keys = tab[n], tab[n + 1]
    chunks = (blocks + per - 1) // per

    def one_chunk(ci, carry):
        load_chunk(tab, kv_in, kv, sems, ci + 1)
        at = pl.ds(ci * per, per)
        pltpu.make_async_copy(kv.at[at], kv.at[at], sems.at[ci]).wait()
        whole = keys >= (ci + 1) * ck

        def both():
            return kv[at, 0].reshape(ck, HD), kv[at, 1].reshape(ck, HD)

        @pl.when(whole)
        def _():
            add_keys(q_ref, *both(), None, acc, m_s, l_s)

        @pl.when(jnp.logical_not(whole))
        def _():
            ok = lax.broadcasted_iota(jnp.int32, (q_ref.shape[0], ck), 1) < keys - ci * ck
            add_keys(q_ref, *both(), ok, acc, m_s, l_s)

        return carry

    lax.fori_loop(0, chunks, one_chunk, 0)


def reset(acc, m_s, l_s):
    acc[...] = jnp.zeros_like(acc)
    l_s[...] = jnp.zeros_like(l_s)
    m_s[...] = jnp.full_like(m_s, NEG)


def write_part(o_ref, st_ref, acc, m_s, l_s):
    heads, tokens, _ = acc.shape
    lane = lax.broadcasted_iota(jnp.int32, (tokens, HD), 1)
    st = jnp.zeros((tokens, HD), jnp.float32)
    for g in range(heads):
        total = jnp.sum(l_s[g], axis=1, keepdims=True)
        inverse = 1.0 / jnp.where(total > 0, total, 1.0)
        o_ref[:, g * HD : (g + 1) * HD] = (acc[g] * inverse).astype(o_ref.dtype)
        st = jnp.where(lane == g, m_s[g], st)
        st = jnp.where(lane == heads + g, total, st)
    st_ref[...] = st.T[: 2 * heads] if st_ref.shape[0] == 2 * heads else st


def begin(tab, q_in, kv_in, q, kv, acc, m_s, l_s, sems):
    copy = pltpu.make_async_copy(q_in, q, sems.at[sems.shape[0] - 1])
    copy.start()
    load_chunk(tab, kv_in, kv, sems, 0)
    reset(acc, m_s, l_s)
    copy.wait()


def partner_kernel(tab, q_in, kv_in, o_ref, st_ref, q, kv, acc, m_s, l_s, sems):
    begin(tab, q_in, kv_in, q, kv, acc, m_s, l_s, sems)
    add_prefix(tab, q, kv_in, kv, acc, m_s, l_s, sems)
    write_part(o_ref, st_ref, acc, m_s, l_s)


def own_kernel(tab, q_in, kv_in, k_ref, v_ref, o_ref, st_ref, q, kv, acc, m_s, l_s, sems):
    begin(tab, q_in, kv_in, q, kv, acc, m_s, l_s, sems)
    tokens = q.shape[0]
    ok = lax.broadcasted_iota(jnp.int32, (tokens, tokens), 1) <= lax.broadcasted_iota(
        jnp.int32, (tokens, tokens), 0
    )
    add_keys(q, k_ref[...], v_ref[...], ok, acc, m_s, l_s)
    add_prefix(tab, q, kv_in, kv, acc, m_s, l_s, sems)
    write_part(o_ref, st_ref, acc, m_s, l_s)


def fold(parts, g, heads):
    m = functools.reduce(jnp.maximum, [m_i for _, m_i, _ in parts])
    shares = [l_i * jnp.exp2((m_i - m) * RATE) for _, m_i, l_i in parts]
    total = functools.reduce(jnp.add, shares)
    inverse = 1.0 / total
    mixed = functools.reduce(jnp.add, [o_i * (w * inverse) for (o_i, _, _), w in zip(parts, shares)])
    return mixed, m, total


def columns(st_ref):
    rows, tokens = st_ref.shape
    return jnp.concatenate([st_ref[...], jnp.zeros((HD - rows, tokens), jnp.float32)], axis=0).T


def stored(o_ref, st, g, heads):
    return (
        o_ref[:, g * HD : (g + 1) * HD].astype(jnp.float32),
        st[:, g : g + 1],
        st[:, heads + g : heads + g + 1],
    )


def merge_kernel(rows, count, oa, sa, ob, sb, *refs):
    outs, out = refs[:-1], refs[-1]
    tokens, width = oa.shape
    heads = width // HD
    ta, tb = columns(sa), sb[...]
    alive = lax.broadcasted_iota(jnp.int32, (tokens, HD), 0) < count[0]
    for g in range(heads):
        mixed, _, _ = fold([stored(oa, ta, g, heads), stored(ob, tb, g, heads)], g, heads)
        out[:, g * HD : (g + 1) * HD] = jnp.where(alive, mixed, 0.0).astype(out.dtype)
    chunk = tokens // (2 * NL)
    per = outs[0].shape[0] // chunk
    for i, o_ref in enumerate(outs):
        for k in range(per):
            o_ref[k * chunk : (k + 1) * chunk] = out[pl.ds(pl.multiple_of(rows[i * per + k] * chunk, chunk), chunk)]


def merge(rows, count, oa, sa, ob, sb):
    tokens, width = oa.shape
    half = jax.ShapeDtypeStruct((tokens // 2, width), jnp.bfloat16)
    return pl.pallas_call(
        merge_kernel,
        out_shape=[half] * 2,
        in_specs=[SM, SM] + [VM] * 4,
        out_specs=[VM] * 2,
        scratch_shapes=[pltpu.VMEM((tokens, width), jnp.bfloat16)],
        compiler_params=SMALL,
        cost_estimate=pl.CostEstimate(flops=8 * tokens * width, bytes_accessed=10 * tokens * width, transcendentals=0),
    )(rows, count, oa, sa, ob, sb)


def state_of(heads, tokens):
    return [pltpu.VMEM((heads, tokens, HD), jnp.float32)] * 3


def attention(body, tab, q, kv, more, more_specs, out_types, params):
    n, bl = tab.shape[0] - 3, kv.shape[2]
    tokens, width = q.shape
    heads = width // HD
    keys = n * bl
    return pl.pallas_call(
        body,
        out_shape=out_types,
        in_specs=[SM, ANY, ANY] + more_specs,
        out_specs=[VM] * len(out_types),
        scratch_shapes=[
            pltpu.VMEM((tokens, width), jnp.bfloat16),
            pltpu.VMEM((n, 2, bl, HD), jnp.bfloat16),
            *state_of(heads, tokens),
            pltpu.SemaphoreType.DMA((max(keys // CK, 1) + 1,)),
        ],
        compiler_params=params,
        cost_estimate=pl.CostEstimate(
            flops=4 * tokens * width * keys, bytes_accessed=keys * HD * 4, transcendentals=tokens * heads * keys
        ),
    )(tab, q, kv, *more)


def project_kernel(x_a, x_b, w_a, w_b, *refs, first):
    (*outs, buf, sems) = refs
    blocks, _, cols = buf.shape

    def copy(c):
        at = pl.ds(pl.multiple_of(c * cols, cols), cols)
        return pltpu.make_async_copy(w_b.at[:, at], buf.at[c], sems.at[c])

    def start(c, carry):
        copy(c).start()
        return carry

    lax.fori_loop(0, blocks, start, 0)
    rows = pl.ds(first, len(outs) * outs[0].shape[0])

    def block(c, carry):
        at = pl.ds(pl.multiple_of(c * cols, cols), cols)
        part = jnp.dot(x_a[rows], w_a[:, at], preferred_element_type=jnp.float32)
        copy(c).wait()
        part = part + jnp.dot(x_b[rows], buf[c], preferred_element_type=jnp.float32)
        chunk = part.shape[0] // len(outs)
        for i, out in enumerate(outs):
            out[:, at] = part[i * chunk : (i + 1) * chunk].astype(out.dtype)
        return carry

    lax.fori_loop(0, blocks, block, 0)


def project(x_a, x_b, w_a, w_b, half, cols=1024):
    rows, depth = x_a.shape
    width = w_a.shape[1]
    return pl.pallas_call(
        functools.partial(project_kernel, first=half * (rows // 2)),
        out_shape=[jax.ShapeDtypeStruct((rows // NL, width), x_a.dtype)] * (NL // 2),
        in_specs=[VM, VM, VM, ANY],
        out_specs=[VM] * (NL // 2),
        scratch_shapes=[
            pltpu.VMEM((width // cols, depth, cols), w_b.dtype),
            pltpu.SemaphoreType.DMA((width // cols,)),
        ],
        compiler_params=SMALL,
        cost_estimate=pl.CostEstimate(
            flops=2 * rows * depth * width, bytes_accessed=4 * depth * width + 2 * rows * width, transcendentals=0
        ),
    )(x_a, x_b, w_a, w_b)


def along_z(hops):
    return [(2 * a + k, 2 * b + k) for a, b in hops for k in range(2)]


def scatter_start(own, for_b, for_ac, for_d):
    from_a = lax.ppermute(for_ac, "tp", along_z([(0, 1), (3, 2)]))
    from_b = lax.ppermute(for_b, "tp", along_z([(0, 2), (3, 1), (1, 0), (2, 3)]))
    from_c = lax.ppermute(for_ac, "tp", along_z([(1, 2), (2, 1)]))
    return [own, for_d, from_a, from_b, from_c]


def scatter_end(own, for_d, from_a, from_b, from_c):
    f32 = jnp.float32
    for_d = (for_d.astype(f32) + from_a.astype(f32)).astype(own.dtype)
    from_d = lax.ppermute(for_d, "tp", along_z([(0, 1), (1, 3), (3, 2), (2, 0)]))
    summed = own.astype(f32) + from_b.astype(f32) + from_c.astype(f32) + from_d.astype(f32)
    return summed.astype(own.dtype)


def local(
    queries,
    new_keys,
    new_values,
    kv_pool,
    out_weight,
    prefix_len,
    new_count,
    hit_holder,
    hit_block,
    decode_owner,
):
    n_pool = lax.axis_size("pool")
    per = hit_holder.shape[1] // n_pool
    tokens, width = queries.shape
    heads = width // HD
    bl = kv_pool.shape[2]
    plane_n = NX * NY
    me = lax.axis_index("pool")
    t_me = lax.axis_index("tp")
    zh = (me // NY) % NZ
    flip = [(p, p ^ NY) for p in range(n_pool)]
    planes = [[(x * NZ + z) * NY + y for x in range(NX) for y in range(NY)] for z in range(NZ)]

    def swap(x, bits):
        return lax.ppermute(x, "tp", [(t, t ^ bits) for t in range(2 * NL)])

    def a2a(x, groups=None):
        return lax.all_to_all(x, "pool", 0, 0, axis_index_groups=groups, tiled=True)

    info = plan(hit_holder, hit_block, prefix_len, new_count, n_pool)
    ids = a2a(info)
    q_far = lax.ppermute(queries, "pool", flip)
    info_far = lax.ppermute(info, "pool", flip)
    w_core = swap(out_weight, 1)
    info_far = lax.ppermute(info, "pool", flip)
    w_core = swap(out_weight, 1)
    x_y = (me // (NZ * NY)) * NY + me % NY
    piece = out_weight.shape[0] // plane_n
    w_piece = swap(lax.dynamic_slice_in_dim(out_weight, x_y * piece, piece, 0), 4)
    w_piece, ids = lax.optimization_barrier((w_piece, ids))
    w_z = lax.all_gather(w_piece, "pool", axis=0, tiled=True, axis_index_groups=planes)

    i = jnp.arange(plane_n, dtype=jnp.int32)
    base = (i // NY) * (NZ * NY) + i % NY
    dest = jnp.stack([base + zh * NY, base + (1 - zh) * NY])
    send_a = gather_blocks(dest, ids, kv_pool, [(1, k) for k in range(per)])
    got_a = a2a(send_a, planes)

    _, owner, count, k_new, v_new, info_far, info = lax.optimization_barrier(
        (send_a, decode_owner[0], new_count, new_keys, new_values, info_far, info)
    )
    keep = (jnp.arange(tokens, dtype=jnp.int32) < count[0])[:, None]
    both = jnp.stack([jnp.where(keep, k_new, 0), jnp.where(keep, v_new, 0)])
    pages = owner.shape[0]
    both = both.reshape(2, pages, PG, HD)
    i = jnp.arange(pages, dtype=jnp.int32)
    page_of = jnp.sum(jnp.where(owner[None, :] == i[:, None], i[None, :], 0), axis=1)
    ordered = jnp.transpose(both[:, page_of], (1, 0, 2, 3)).reshape(NX, NZ, NY, 2 * PG, HD)
    near = lax.dynamic_index_in_dim(ordered, zh, 1, keepdims=False).reshape(plane_n, 2 * PG, HD)
    away = lax.dynamic_index_in_dim(ordered, 1 - zh, 1, keepdims=False).reshape(plane_n, 2 * PG, HD)
    away = lax.ppermute(away, "pool", flip)

    send_b = gather_blocks(dest, ids, kv_pool, [(0, k) for k in range(per)], (near, away))
    tab_far = block_table(info_far, zh, per, (0, per), bl)
    tab = block_table(info, zh, per, (0, per), bl)
    send_b, q_far, w_core, tab_far, tab = lax.optimization_barrier((send_b, q_far, w_core, tab_far, tab))
    got_b = a2a(send_b, planes)

    st_type = jax.ShapeDtypeStruct((2 * heads, tokens), jnp.float32)
    st_wide = jax.ShapeDtypeStruct((tokens, HD), jnp.float32)
    o_type = jax.ShapeDtypeStruct((tokens, width), jnp.bfloat16)
    o_wide = jax.ShapeDtypeStruct((tokens, width), jnp.float32)
    o_a, st_a = attention(partner_kernel, tab_far, q_far, got_a, (), [], [o_type, st_type], LARGE)
    o_a, st_a = lax.ppermute(o_a, "pool", flip), lax.ppermute(st_a, "pool", flip)
    o_b, st_b = attention(own_kernel, tab, queries, got_b, (k_new, v_new), [VM] * 2, [o_wide, st_wide], SMALL)

    core, j = t_me % 2, t_me // 2
    mine = 2 * jnp.array(SENDS, jnp.int32)[j]
    rows = jnp.concatenate([mine + core, mine + 1 - core])
    x_keep, x_give = merge(rows, new_count, o_a, st_a, o_b, st_b)
    x = (x_keep, swap(x_give, 1), out_weight, w_core)
    for_b, for_ac = project(*x, 0)
    own, for_d = project(*x, 1)
    summed = scatter_end(*scatter_start(own, for_b, for_ac, for_d))

    arrived = got_b[:, 2 * per].reshape(NX, NY, 2, 2 * PG, HD)
    near_in, far_in = arrived[:, :, 0], arrived[:, :, 1]
    by_z = jnp.where(zh == 0, jnp.stack([near_in, far_in], 1), jnp.stack([far_in, near_in], 1))
    decode = by_z.reshape(n_pool, 1, 2, PG, HD)[None]
    return (summed, decode)


def solution(mesh):
    in_specs = (
        P("pool", "tp"),
        P("pool", "tp"),
        P("pool", "tp"),
        P("pool", None, None, "tp"),
        P("tp", None),
        P("pool"),
        P("pool"),
        P("pool", None),
        P("pool", None),
        P("pool", None),
    )
    out_specs = (P(("pool", "tp"), None), P("pool", None, None, None, None, "tp"))
    return jax.shard_map(local, mesh=mesh, in_specs=in_specs, out_specs=out_specs, check_vma=False)
```
